512 devices in a mesh: seq: 64 (over x, z), ch: 8 (over y, core).
Axes of the slice: x: 4, y: 4, z: 16, core: 2. Of those that a mesh axis runs over, the one named last changes fastest.
Arguments:
- stream_one: bfloat16 [8192, 2048], P('seq', 'ch'), may hold values from -6 to 6
- stream_two: bfloat16 [8192, 2048], P('seq', 'ch'), may hold values from -6 to 6
- stream_value: bfloat16 [8192, 2048], P('seq', 'ch'), may hold values from -6 to 6
- long_filter: bfloat16 [8192, 2048], P('seq', 'ch'), may hold values from -4 to 4
- short_taps: float32 [3, 3, 2048], P(None, None, 'ch'), may hold values from -3.5 to 3.5
- skip_gain: float32 [2048], P('ch'), may hold values from -1 to 1
- out_grad: bfloat16 [8192, 2048], P('seq', 'ch'), may hold values from -0.59765625 to 0.59765625
Outputs:
- mixed_out: bfloat16 [8192, 2048], P('seq', 'ch')
- grad_one: bfloat16 [8192, 2048], P('seq', 'ch')
- grad_two: bfloat16 [8192, 2048], P('seq', 'ch')
- grad_value: bfloat16 [8192, 2048], P('seq', 'ch')
- grad_filter: float32 [8192, 2048], P('seq', 'ch')
- grad_taps: float32 [3, 3, 2048], P(None, None, 'ch')
- grad_skip: float32 [2048], P('ch')
The draws below stay inside these ranges and needn't reach their ends.
All inputs are finite; a program needn't handle non-finite values.
Results may differ from the reference program's by a relative error of at most 0.0054.
Values may be sent and summed in bfloat16 or wider, within the bound.
A program may use at most 64 MiB of HBM per device.

```python
import math
import jax
import jax.numpy as jnp
from jax import lax

HALF_MODEL_DIMS = 2048
TAPS = 3
STEP_COUNT = 8192
FFT_LEN = 16384


def draw_long_filter(key, part):
    key_noise = jax.random.fold_in(key, 11)
    key_rate = jax.random.fold_in(key, 12)
    placement_seed = jax.random.fold_in(key, 13)
    keeping_generator_start = jax.random.fold_in(key, 14)
    delay_ratio = jnp.arange(STEP_COUNT, dtype=jnp.float32)[:, None] / STEP_COUNT
    damping_rates = jnp.exp(jax.random.uniform(key_rate, (1, HALF_MODEL_DIMS), jnp.float32, math.log(0.02), math.log(200.0)))
    random_draws = jnp.clip(jax.random.normal(key_noise, (STEP_COUNT, HALF_MODEL_DIMS), jnp.float32), -4.0, 4.0)
    spike_shift_amount = jax.random.randint(placement_seed, (3, 1, HALF_MODEL_DIMS), 1, STEP_COUNT)
    spike_kept_mask = jax.random.uniform(keeping_generator_start, (3, 1, HALF_MODEL_DIMS), jnp.float32, 0.5, 0.8)
    chosen_slot_list = jnp.arange(STEP_COUNT, dtype=jnp.int32)[:, None]
    spike_shape_curve = jnp.ones((STEP_COUNT, HALF_MODEL_DIMS), jnp.float32)
    for spike_chooser in range(3):
        spike_shape_curve = spike_shape_curve * jnp.where(chosen_slot_list >= spike_shift_amount[spike_chooser], spike_kept_mask[spike_chooser], 1.0)
    magnitude_divisor = jnp.sqrt(2.0 * damping_rates / (STEP_COUNT * (1.0 - jnp.exp(-2.0 * damping_rates))))
    return (random_draws * jnp.exp(-damping_rates * delay_ratio) * spike_shape_curve * magnitude_divisor).astype(jnp.bfloat16)


def steps_of(own_key, dims, cuts, low, top_value):
    def one(axis_at, blocks):
        heights = jax.random.uniform(jax.random.fold_in(jax.random.fold_in(own_key, 6), axis_at), (blocks,), jnp.float32, low / len(cuts), top_value / len(cuts))
        return jnp.repeat(jnp.exp(heights), dims[axis_at] // blocks).reshape((-1,) + (1,) * (len(dims) - axis_at - 1))

    gain = one(*cuts[0])
    for cut in cuts[1:]:
        gain = gain * one(*cut)
    return gain


def gaussian(key, shape, width, limit, cuts=(), kind=jnp.bfloat16):
    drawn = width * jax.random.normal(key, shape, jnp.float32)
    if cuts:
        drawn = drawn * steps_of(key, shape, cuts, -0.22, 0.18)
    return jnp.clip(drawn, -limit, limit).astype(kind)


def setup_inputs(seed: int = 0) -> dict:
    keys = jax.random.split(jax.random.key(seed), 8)
    return {
        "stream_one": gaussian(keys[0], (STEP_COUNT, HALF_MODEL_DIMS), 1.0, 6.0, ((0, 64), (1, 8))),
        "stream_two": gaussian(keys[1], (STEP_COUNT, HALF_MODEL_DIMS), 1.0, 6.0, ((0, 64), (1, 8))),
        "stream_value": gaussian(keys[2], (STEP_COUNT, HALF_MODEL_DIMS), 1.0, 6.0, ((0, 64), (1, 8))),
        "long_filter": draw_long_filter(jax.random.fold_in(keys[7], 71), 0),
        "short_taps": gaussian(keys[4], (3, TAPS, HALF_MODEL_DIMS), TAPS ** -0.5, 3.5, ((2, 8),), jnp.float32),
        "skip_gain": jnp.clip(jax.random.uniform(keys[5], (HALF_MODEL_DIMS,), jnp.float32, -1.0, 1.0) * steps_of(keys[5], (HALF_MODEL_DIMS,), ((0, 8),), -0.4, 0.0), -1.0, 1.0),
        "out_grad": gaussian(keys[6], (STEP_COUNT, HALF_MODEL_DIMS), 0.1, 0.59765625, ((0, 64), (1, 8))),
    }


def short_filter(streams, short_taps):
    tap_count = short_taps.shape[1]
    padded = jnp.pad(streams, ((0, 0), (tap_count - 1, 0), (0, 0)))
    summed = jnp.zeros_like(streams)
    for offset in range(tap_count):
        first_row = tap_count - 1 - offset
        summed = summed + short_taps[:, offset, None, :] * padded[:, first_row:first_row + STEP_COUNT]
    return summed, padded


def causal_mix(signal, kernel):
    product = jnp.fft.rfft(signal, n=FFT_LEN, axis=0) * jnp.fft.rfft(kernel, n=FFT_LEN, axis=0)
    return jnp.fft.irfft(product, n=FFT_LEN, axis=0)[:STEP_COUNT].astype(jnp.float32)


def causal_match(signal, kernel):
    product = jnp.fft.rfft(signal, n=FFT_LEN, axis=0) * jnp.conj(jnp.fft.rfft(kernel, n=FFT_LEN, axis=0))
    return jnp.fft.irfft(product, n=FFT_LEN, axis=0)[:STEP_COUNT].astype(jnp.float32)


def reference(stream_one, stream_two, stream_value, long_filter, short_taps, skip_gain, out_grad):
    streams = jnp.stack([stream_one, stream_two, stream_value]).astype(jnp.float32)
    convolved, padded = short_filter(streams, short_taps)
    gate_out, gate_in, value_conv = convolved[0], convolved[1], convolved[2]
    cotangent = out_grad.astype(jnp.float32)
    mixed_in = lax.optimization_barrier((gate_in * value_conv).astype(jnp.bfloat16)).astype(jnp.float32)
    back_grad = lax.optimization_barrier((cotangent * gate_out).astype(jnp.bfloat16)).astype(jnp.float32)
    filter_wide = long_filter.astype(jnp.float32)
    long_out = causal_mix(mixed_in, filter_wide) + skip_gain * mixed_in
    mixed_out = (gate_out * long_out).astype(jnp.bfloat16)
    grad_filter = causal_match(back_grad, mixed_in)
    grad_mixed_in = causal_match(back_grad, filter_wide) + skip_gain * back_grad
    grad_skip = jnp.sum(back_grad * mixed_in, axis=0)
    conv_grads = jnp.stack([cotangent * long_out, grad_mixed_in * value_conv, grad_mixed_in * gate_in])
    tap_count = short_taps.shape[1]
    taps_list = []
    for offset in range(tap_count):
        first_row = tap_count - 1 - offset
        taps_list.append(jnp.sum(conv_grads * padded[:, first_row:first_row + STEP_COUNT], axis=1))
    grad_taps = jnp.stack(taps_list, axis=1)
    trailing = jnp.pad(conv_grads, ((0, 0), (0, tap_count - 1), (0, 0)))
    grad_streams = jnp.zeros_like(conv_grads)
    for offset in range(tap_count):
        grad_streams = grad_streams + short_taps[:, offset, None, :] * trailing[:, offset:offset + STEP_COUNT]
    grad_streams = grad_streams.astype(jnp.bfloat16)
    return (mixed_out, grad_streams[0], grad_streams[1], grad_streams[2], grad_filter, grad_taps, grad_skip)
```

```python
import functools
import math

import jax
import jax.numpy as jnp
import numpy as np
from jax import lax
from jax.experimental import pallas as pl
from jax.experimental.pallas import tpu as pltpu
from jax.sharding import PartitionSpec as P

MESH = pl.DeviceIdType.MESH
F32 = jnp.float32
BF16 = jnp.bfloat16


def halves(table):
    high = table.astype(BF16)
    low = (table - high.astype(np.float64)).astype(BF16)
    return high, low


def tables(devices, tokens, own):
    length = 2 * devices * tokens
    a = np.arange(devices)
    b = np.arange(tokens)
    odd = np.arange(devices) + 0.5
    outer = 2 * math.pi * np.outer(odd, a) / (2 * devices)
    first = np.concatenate([np.cos(outer), -np.sin(outer)], 0)
    last = np.concatenate([np.cos(outer.T), np.sin(outer.T)], 1) * (2.0 / length)
    turn = 2 * math.pi * np.outer(odd, b) / length
    inner = 2 * math.pi * (np.outer(b, b) % tokens) / tokens
    cosine, sine = np.cos(inner), np.sin(inner)
    second = np.block([[cosine, -sine], [sine, cosine]])
    order = np.zeros((own * devices, own * devices))
    for c in range(own):
        order[c * devices + a, a * own + c] = 1.0
    first_high, first_low = halves(first)
    return (
        np.concatenate([first_high, first_low], 0),
        np.stack(halves(last)),
        np.cos(turn).astype(np.float32),
        (-np.sin(turn)).astype(np.float32),
        np.stack(halves(second)),
        order.astype(BF16),
        order.T.astype(BF16),
    )


def split(x):
    high = x.astype(BF16)
    return high, (x - high.astype(F32)).astype(BF16)


def mul(a, b):
    return jnp.dot(a, b, preferred_element_type=F32)


def exchange_kernel(
    devices, own, one_ref, two_ref, value_ref, filter_ref, cot_ref, taps_ref, skip_ref,
    first_ref, last_ref, turn_re_ref, turn_im_ref, second_ref, order_ref, back_ref,
    out_ref, sums_ref,
    send, recv, ret, sums, send_sem, recv_sem, ret_sem, out_sem, sums_sems,
):
    me = lax.axis_index("seq")
    tokens = one_ref.shape[0]
    barrier = pltpu.get_barrier_semaphore()

    def greet(k, carry):
        pl.semaphore_signal(
            barrier, inc=1, device_id={"seq": lax.rem(me + k, devices)}, device_id_type=MESH
        )
        return carry

    lax.fori_loop(1, devices, greet, 0)

    sources = (filter_ref, two_ref, value_ref, one_ref, cot_ref)
    count = len(sources)

    def pack(p):
        send[p] = sources[p][...].T.reshape(devices, own, tokens)

    def spread(p, src, dst, ssem, rsem):
        def body(k, carry):
            d = lax.rem(me + k, devices)
            pltpu.make_async_remote_copy(
                src.at[p, d], dst.at[p, me], ssem.at[p], rsem.at[p],
                device_id={"seq": d}, device_id_type=MESH,
            ).start()
            return carry

        lax.fori_loop(1, devices, body, 0)
        pltpu.make_async_copy(src.at[p, me], dst.at[p, me], rsem.at[p]).start()

    for p in range(count):
        pack(p)
    pl.semaphore_wait(barrier, devices - 1)
    for p in range(count):
        spread(p, send, recv, send_sem, recv_sem)

    def arrive(p):
        pltpu.make_async_copy(recv.at[p], recv.at[p], recv_sem.at[p]).wait()
        got = mul(order_ref[...], recv[p].reshape(devices * own, tokens))
        return [got[c * devices : (c + 1) * devices] for c in range(own)]

    lane = lax.broadcasted_iota(jnp.int32, (devices, tokens), 1)
    row = lax.broadcasted_iota(jnp.int32, (devices, tokens), 0)

    def later(x, j):
        r = pltpu.roll(x, j, 1)
        up = jnp.where(row == 0, 0.0, pltpu.roll(r, 1, 0))
        return jnp.where(lane < j, up, r)

    def sooner(x, j):
        r = pltpu.roll(x, tokens - j, 1)
        down = jnp.where(row == devices - 1, 0.0, pltpu.roll(r, devices - 1, 0))
        return jnp.where(lane >= tokens - j, down, r)

    def tap(s, j, c):
        return taps_ref[3 * s + j, own * me + c]

    def short(s, c, x):
        moved = (x, later(x, 1), later(x, 2))
        total = tap(s, 0, c) * moved[0]
        total = total + tap(s, 1, c) * moved[1]
        return total + tap(s, 2, c) * moved[2], moved

    turn_re, turn_im = turn_re_ref[...], turn_im_ref[...]
    second_high, second_low = second_ref[0], second_ref[1]

    def rotate(re, im):
        return re * turn_re - im * turn_im, re * turn_im + im * turn_re

    def mul_second(x):
        high, low = split(x)
        return mul(high, second_high) + (mul(low, second_high) + mul(high, second_low))

    def forward(parts):
        rows = []
        for x in parts:
            both = mul(first_ref[...], x)
            both = both[: 2 * devices] + both[2 * devices :]
            rows.append(jnp.concatenate(rotate(both[:devices], both[devices:]), 1))
        full = mul_second(jnp.concatenate(rows, 0))
        return full[:, :tokens], full[:, tokens:]

    def inverse(re, im):
        full = mul_second(jnp.concatenate([re, im], 1))
        result = []
        for c in range(own):
            part = full[c * devices : (c + 1) * devices]
            high, low = split(jnp.concatenate(rotate(part[:, :tokens], part[:, tokens:]), 0))
            result.append(mul(last_ref[0], high) + (mul(last_ref[0], low) + mul(last_ref[1], high)))
        return result

    filt = [x.astype(BF16) for x in arrive(0)]
    filt_re, filt_im = forward(filt)
    two = [short(1, c, x) for c, x in enumerate(arrive(1))]
    val = [short(2, c, x) for c, x in enumerate(arrive(2))]
    mixed = [(two[c][0] * val[c][0]).astype(BF16) for c in range(own)]
    mix_re, mix_im = forward(mixed)
    conv = inverse(mix_re * filt_re - mix_im * filt_im, -(mix_re * filt_im + mix_im * filt_re))
    one = [short(0, c, x) for c, x in enumerate(arrive(3))]
    cot = arrive(4)
    back = [(cot[c] * one[c][0]).astype(BF16) for c in range(own)]
    back_re, back_im = forward(back)
    grad_filter = inverse(
        back_re * mix_re + back_im * mix_im, back_re * mix_im - back_im * mix_re
    )
    grad_mixed = inverse(
        back_re * filt_re + back_im * filt_im, back_re * filt_im - back_im * filt_re
    )

    def give(p, parts):
        stacked = jnp.concatenate([x.astype(BF16) for x in parts], 0)
        ret[p] = mul(back_ref[...], stacked).astype(BF16).reshape(devices, own, tokens)
        spread(p, ret, out_ref, ret_sem, out_sem)

    give(4, grad_filter)
    gathered = []
    outs = [[], [], [], []]
    for c in range(own):
        skip = skip_ref[0, own * me + c]
        mixed_wide, back_wide = mixed[c].astype(F32), back[c].astype(F32)
        long_out = conv[c] + skip * mixed_wide
        grad_in = grad_mixed[c] + skip * back_wide
        outs[0].append(one[c][0] * long_out)
        grads = (cot[c] * long_out, grad_in * val[c][0], grad_in * two[c][0])
        streams = (one[c][1], two[c][1], val[c][1])
        sections = []
        for s in range(3):
            total = tap(s, 0, c) * grads[s]
            total = total + tap(s, 1, c) * sooner(grads[s], 1)
            outs[1 + s].append(total + tap(s, 2, c) * sooner(grads[s], 2))
            for j in range(3):
                sections.append(grads[s] * streams[s][j])
        sections.append(back_wide * mixed_wide)
        for x in sections:
            gathered.append(x.reshape(devices // 8, 8, tokens).sum(0))
        for _ in range(6):
            gathered.append(jnp.zeros((8, tokens), F32))
    for p in range(4):
        give(p, outs[p])
    high, low = split(jnp.concatenate(gathered, 0))
    ones = jnp.ones((tokens, tokens), BF16)
    totals = mul(high, ones) + mul(low, ones)
    shape = totals.shape
    pick = lax.broadcasted_iota(jnp.int32, shape, 0) // 8 == lax.broadcasted_iota(jnp.int32, shape, 1)
    sums[...] = jnp.where(pick, totals, 0.0).sum(0, keepdims=True)

    def tell(k, carry):
        d = lax.rem(me + k, devices)
        pltpu.make_async_remote_copy(
            sums, sums_ref.at[me], sums_sems.at[0], sums_sems.at[1],
            device_id={"seq": d}, device_id_type=MESH,
        ).start()
        return carry

    lax.fori_loop(1, devices, tell, 0)
    pltpu.make_async_copy(sums, sums_ref.at[me], sums_sems.at[1]).start()

    others = pl.ds(0, devices - 1)
    for p in range(count):
        pltpu.make_async_copy(send.at[p, others], send.at[p, others], send_sem.at[p]).wait()
        pltpu.make_async_copy(ret.at[p, others], ret.at[p, others], ret_sem.at[p]).wait()
    for p in range(count):
        pltpu.make_async_copy(out_ref.at[p], out_ref.at[p], out_sem.at[p]).wait()
    pltpu.make_async_copy(sums_ref.at[others], sums_ref.at[others], sums_sems.at[0]).wait()
    pltpu.make_async_copy(sums_ref, sums_ref, sums_sems.at[1]).wait()


def finish_kernel(
    got_ref, sums_ref, mixed_out_ref, one_ref, two_ref, value_ref, filter_ref, taps_ref, skip_ref
):
    _, devices, own, tokens = got_ref.shape
    for p, ref in enumerate((mixed_out_ref, one_ref, two_ref, value_ref, filter_ref)):
        ref[...] = got_ref[p].reshape(devices * own, tokens).T.astype(ref.dtype)
    turned = sums_ref[...].reshape(devices, tokens).T
    source = lax.broadcasted_iota(jnp.int32, (devices, devices * own), 0)
    target = lax.broadcasted_iota(jnp.int32, (devices, devices * own), 1)
    total = jnp.zeros((16, devices * own), F32)
    for c in range(own):
        place = jnp.where(target == source * own + c, 1.0, 0.0)
        total = total + jnp.dot(
            turned[16 * c : 16 * (c + 1)], place,
            precision=lax.Precision.HIGHEST, preferred_element_type=F32,
        )
    taps_ref[...] = total[:9]
    skip_ref[...] = total[9:10]


def per_device(one, two, value, long_filter, short_taps, skip_gain, out_grad):
    devices = lax.axis_size("seq")
    tokens, channels = one.shape
    own = channels // devices
    vmem = pl.BlockSpec(memory_space=pltpu.VMEM)
    smem = pl.BlockSpec(memory_space=pltpu.SMEM)
    consts = [jnp.asarray(t) for t in tables(devices, tokens, own)]
    blocks = (5, devices, own, tokens)
    got, sums = pl.pallas_call(
        functools.partial(exchange_kernel, devices, own),
        out_shape=(
            jax.ShapeDtypeStruct(blocks, BF16),
            jax.ShapeDtypeStruct((devices, 1, tokens), F32),
        ),
        in_specs=[vmem] * 5 + [smem] * 2 + [vmem] * len(consts),
        out_specs=(vmem, vmem),
        scratch_shapes=[
            pltpu.VMEM(blocks, BF16),
            pltpu.VMEM(blocks, BF16),
            pltpu.VMEM(blocks, BF16),
            pltpu.VMEM((1, tokens), F32),
            pltpu.SemaphoreType.DMA((5,)),
            pltpu.SemaphoreType.DMA((5,)),
            pltpu.SemaphoreType.DMA((5,)),
            pltpu.SemaphoreType.DMA((5,)),
            pltpu.SemaphoreType.DMA((2,)),
        ],
        compiler_params=pltpu.CompilerParams(
            collective_id=0, has_side_effects=True, vmem_limit_bytes=40 * 1024 * 1024
        ),
        name="exchange",
    )(
        one, two, value, long_filter, out_grad,
        short_taps.reshape(9, channels), skip_gain.reshape(1, channels), *consts,
    )
    full = jax.ShapeDtypeStruct((tokens, channels), BF16)
    *outs, taps, skip = pl.pallas_call(
        finish_kernel,
        out_shape=(
            full, full, full, full,
            jax.ShapeDtypeStruct((tokens, channels), F32),
            jax.ShapeDtypeStruct((9, channels), F32),
            jax.ShapeDtypeStruct((1, channels), F32),
        ),
        in_specs=[vmem] * 2,
        out_specs=(vmem,) * 7,
        name="finish",
    )(got, sums)
    return (*outs, taps.reshape(3, 3, channels), skip.reshape(channels))


def solution(mesh):
    rows, lanes = P("seq", "ch"), P("ch")
    taps = P(None, None, "ch")
    return jax.shard_map(
        per_device,
        mesh=mesh,
        in_specs=(rows, rows, rows, rows, taps, lanes, rows),
        out_specs=(rows, rows, rows, rows, rows, taps, lanes),
        check_vma=False,
    )
```

```python
import functools
import math

import jax
import jax.numpy as jnp
import numpy as np
from jax import lax
from jax.experimental import pallas as pl
from jax.experimental.pallas import tpu as pltpu
from jax.sharding import PartitionSpec as P

MESH = pl.DeviceIdType.MESH
F32 = jnp.float32
BF16 = jnp.bfloat16
LANES = 128
HALO_LATER, HALO_SOONER, SUMS, FIELD = 0, 6, 12, 32


def halves(table):
    high = table.astype(BF16)
    low = (table - high.astype(np.float64)).astype(BF16)
    return high, low


def tables(devices, tokens, own):
    length = 2 * devices * tokens
    a = np.arange(devices)
    b = np.arange(tokens)
    odd = np.arange(devices) + 0.5
    outer = 2 * math.pi * np.outer(odd, a) / (2 * devices)
    first = np.concatenate([np.cos(outer), -np.sin(outer)], 0)
    last = np.concatenate([np.cos(outer.T), np.sin(outer.T)], 1) * (2.0 / length)
    turn = 2 * math.pi * np.outer(odd, b) / length
    inner = 2 * math.pi * (np.outer(b, b) % tokens) / tokens
    cosine, sine = np.cos(inner), np.sin(inner)
    second = np.block([[cosine, -sine], [sine, cosine]])
    order = np.zeros((own * devices, own * devices))
    for c in range(own):
        order[c * devices + a, a * own + c] = 1.0
    return (
        np.concatenate(halves(first), 0),
        np.stack(halves(last)),
        np.stack([np.cos(turn), -np.sin(turn)]).astype(np.float32),
        np.stack(halves(second)),
        np.stack([order, order.T]).astype(BF16),
    )


def split(x):
    high = x.astype(BF16)
    return high, (x - high.astype(F32)).astype(BF16)


def mul(a, b):
    return jnp.dot(a, b, preferred_element_type=F32)


def exchange_kernel(
    devices, parts, own,
    filter_in, two_in, value_in, one_in, cot_in, first_in, last_in, turn_in, second_in, order_in,
    taps_ref, skip_ref,
    out_ref, edge_ref,
    filter_ref, two_ref, value_ref, one_ref, cot_ref,
    first_ref, last_ref, turn_ref, second_ref, order_ref,
    send, recv, ret, edge,
    load_sem, send_sem, recv_sem, ret_sem, out_sem, edge_sem,
):
    me = lax.axis_index("seq")
    tokens = filter_ref.shape[0]
    barrier = pltpu.get_barrier_semaphore()
    inputs = (filter_in, two_in, value_in, one_in, cot_in, first_in, last_in, turn_in, second_in, order_in)
    held = (filter_ref, two_ref, value_ref, one_ref, cot_ref, first_ref, last_ref, turn_ref, second_ref, order_ref)
    loads = [pltpu.make_async_copy(x, y, load_sem.at[i]) for i, (x, y) in enumerate(zip(inputs, held))]
    for load in loads:
        load.start()

    def greet(k, carry):
        pl.semaphore_signal(
            barrier, inc=1, device_id={"seq": lax.rem(me + k, devices)}, device_id_type=MESH
        )
        return carry

    lax.fori_loop(1, devices, greet, 0)

    def spread(src, dst, ssem, rsem):
        def body(k, carry):
            d = lax.rem(me + k, devices)
            pltpu.make_async_remote_copy(
                src.at[d], dst.at[me], ssem, rsem, device_id={"seq": d}, device_id_type=MESH
            ).start()
            return carry

        lax.fori_loop(1, devices, body, 0)
        pltpu.make_async_copy(src.at[me], dst.at[me], rsem).start()

    for p in range(5):
        loads[p].wait()
        for h in range(parts):
            block = held[p][:, h * LANES : (h + 1) * LANES].T
            send[h, :, p] = block.reshape(devices, own, tokens)
    pl.semaphore_wait(barrier, devices - 1)
    for h in range(parts):
        spread(send.at[h], recv.at[h], send_sem.at[h], recv_sem.at[h])
    for load in loads[5:]:
        load.wait()

    lane = lax.broadcasted_iota(jnp.int32, (devices, tokens), 1)
    row = lax.broadcasted_iota(jnp.int32, (devices, tokens), 0)

    def later(x, j):
        r = pltpu.roll(x, j, 1)
        up = jnp.where(row == 0, 0.0, pltpu.roll(r, 1, 0))
        return jnp.where(lane < j, up, r)

    def tap(s, j, channel):
        return taps_ref[s, j, channel]

    def short(s, channel, x):
        moved = (x, later(x, 1), later(x, 2))
        total = tap(s, 0, channel) * moved[0]
        total = total + tap(s, 1, channel) * moved[1]
        return total + tap(s, 2, channel) * moved[2], moved

    turn_re, turn_im = turn_ref[0], turn_ref[1]

    def rotate(re, im):
        return re * turn_re - im * turn_im, re * turn_im + im * turn_re

    def mul_second(x):
        high, low = split(x)
        return mul(high, second_ref[0]) + (mul(low, second_ref[0]) + mul(high, second_ref[1]))

    def rows_of(x, i):
        return x[i * devices : (i + 1) * devices]

    def forward(pieces):
        rows = []
        for x in pieces:
            both = mul(first_ref[...], x)
            both = both[: 2 * devices] + both[2 * devices :]
            rows.append(jnp.concatenate(rotate(both[:devices], both[devices:]), 1))
        full = mul_second(jnp.concatenate(rows, 0))
        size = own * devices
        return [
            (full[i * size : (i + 1) * size, :tokens], full[i * size : (i + 1) * size, tokens:])
            for i in range(len(pieces) // own)
        ]

    def inverse(spectra):
        full = mul_second(jnp.concatenate([jnp.concatenate(z, 1) for z in spectra], 0))
        result = []
        for i in range(len(spectra) * own):
            part = rows_of(full, i)
            high, low = split(jnp.concatenate(rotate(part[:, :tokens], part[:, tokens:]), 0))
            result.append(mul(last_ref[0], high) + (mul(last_ref[0], low) + mul(last_ref[1], high)))
        return [result[i * own : (i + 1) * own] for i in range(len(spectra))]

    edges = jnp.zeros((devices, tokens), F32)
    sums = jnp.zeros((1, tokens), F32)
    ones = jnp.ones((tokens, tokens), BF16)
    for h in range(parts):
        pltpu.make_async_copy(recv.at[h], recv.at[h], recv_sem.at[h]).wait()
        got = []
        for p in range(5):
            x = mul(order_ref[0], recv[h, :, p].reshape(devices * own, tokens))
            got.append([rows_of(x, c) for c in range(own)])
        channels = [h * LANES + own * me + c for c in range(own)]
        filt = [x.astype(BF16) for x in got[0]]
        two = [short(1, channels[c], got[1][c]) for c in range(own)]
        val = [short(2, channels[c], got[2][c]) for c in range(own)]
        one = [short(0, channels[c], got[3][c]) for c in range(own)]
        cot = got[4]
        mixed = [(two[c][0] * val[c][0]).astype(BF16) for c in range(own)]
        back = [(cot[c] * one[c][0]).astype(BF16) for c in range(own)]
        (f_re, f_im), (m_re, m_im), (b_re, b_im) = forward(filt + mixed + back)
        conv, grad_mixed, grad_filter = inverse([
            (m_re * f_re - m_im * f_im, -(m_re * f_im + m_im * f_re)),
            (b_re * f_re + b_im * f_im, b_re * f_im - b_im * f_re),
            (b_re * m_re + b_im * m_im, b_re * m_im - b_im * m_re),
        ])
        wide = []
        for c in range(own):
            skip = skip_ref[channels[c]]
            mixed_wide, back_wide = mixed[c].astype(F32), back[c].astype(F32)
            wide.append((mixed_wide, back_wide, conv[c] + skip * mixed_wide, grad_mixed[c] + skip * back_wide))
        for p, pieces in enumerate(([w[2] for w in wide], [w[3] for w in wide], grad_filter)):
            stacked = jnp.concatenate([x.astype(BF16) for x in pieces], 0)
            ret[h, :, p] = mul(order_ref[1], stacked).astype(BF16).reshape(devices, own, tokens)
        spread(ret.at[h], out_ref.at[h], ret_sem.at[h], out_sem.at[h])

        sections = []
        for c in range(own):
            mixed_wide, back_wide, long_out, grad_in = wide[c]
            grads = (cot[c] * long_out, grad_in * val[c][0], grad_in * two[c][0])
            streams = (one[c][1], two[c][1], val[c][1])
            start = FIELD * (h * own + c)
            for s in range(3):
                at = start + HALO_LATER + 2 * s
                piece = pltpu.roll(streams[s][2], at, 1) if at else streams[s][2]
                edges = jnp.where((lane >= at) & (lane < at + 2), piece, edges)
                at = start + HALO_SOONER + 2 * s
                ahead = jnp.where(row == devices - 1, 0.0, pltpu.roll(grads[s], devices - 1, 0))
                edges = jnp.where((lane >= at) & (lane < at + 2), pltpu.roll(ahead, at, 1), edges)
                for j in range(3):
                    sections.append(grads[s] * streams[s][j])
            sections.append(back_wide * mixed_wide)
            sections += [None] * 6
        gathered = [
            jnp.zeros((8, tokens), F32) if x is None else x.reshape(devices // 8, 8, tokens).sum(0)
            for x in sections
        ]
        high, low = split(jnp.concatenate(gathered, 0))
        totals = mul(high, ones) + mul(low, ones)
        section = lax.broadcasted_iota(jnp.int32, totals.shape, 0) // 8
        target = FIELD * (h * own + section // 16) + SUMS + section % 16
        pick = lax.broadcasted_iota(jnp.int32, totals.shape, 1) == target
        sums = sums + jnp.where(pick, totals, 0.0).sum(0, keepdims=True)

    edge[...] = (edges + sums).reshape(devices, 1, tokens)
    spread(edge, edge_ref, edge_sem.at[0], edge_sem.at[1])

    others = pl.ds(0, devices - 1)

    def settle(ref, sem):
        pltpu.make_async_copy(ref, ref, sem).wait()

    for h in range(parts):
        settle(send.at[h, others], send_sem.at[h])
        settle(ret.at[h, others], ret_sem.at[h])
        settle(out_ref.at[h], out_sem.at[h])
    settle(edge.at[others], edge_sem.at[0])
    settle(edge_ref, edge_sem.at[1])


def finish_kernel(
    got_ref, edge_ref, one_ref, two_ref, value_ref, cot_ref, taps_ref,
    mixed_out_ref, grad_one_ref, grad_two_ref, grad_value_ref, filter_ref, taps_out_ref, skip_out_ref,
):
    parts, devices, _, own, tokens = got_ref.shape
    turned = edge_ref[...].reshape(devices, tokens).T
    source = lax.broadcasted_iota(jnp.int32, (devices, LANES), 0)
    target = lax.broadcasted_iota(jnp.int32, (devices, LANES), 1)
    row = lax.broadcasted_iota(jnp.int32, (tokens, LANES), 0)
    for h in range(parts):
        at = slice(h * LANES, (h + 1) * LANES)
        edges = jnp.zeros((FIELD, LANES), F32)
        for c in range(own):
            place = jnp.where(target == source * own + c, 1.0, 0.0)
            start = FIELD * (h * own + c)
            edges = edges + jnp.dot(
                turned[start : start + FIELD], place,
                precision=lax.Precision.HIGHEST, preferred_element_type=F32,
            )

        def edge(i):
            return edges[i : i + 1]

        def tap(s, j):
            return taps_ref[s, j : j + 1, at]

        long_out, grad_in, grad_filter = [
            got_ref[h, :, p].reshape(LANES, tokens).T.astype(F32) for p in range(3)
        ]
        gates = []
        for s, ref in enumerate((one_ref, two_ref, value_ref)):
            x = ref[:, at].astype(F32)
            i = HALO_LATER + 2 * s
            once = jnp.where(row == 0, edge(i + 1), pltpu.roll(x, 1, 0))
            twice = jnp.where(row == 0, edge(i), jnp.where(row == 1, edge(i + 1), pltpu.roll(x, 2, 0)))
            total = tap(s, 0) * x
            total = total + tap(s, 1) * once
            gates.append(total + tap(s, 2) * twice)
        mixed_out_ref[:, at] = (gates[0] * long_out).astype(BF16)
        grads = (cot_ref[:, at].astype(F32) * long_out, grad_in * gates[2], grad_in * gates[1])
        for s, ref in enumerate((grad_one_ref, grad_two_ref, grad_value_ref)):
            x = grads[s]
            i = HALO_SOONER + 2 * s
            once = jnp.where(row == tokens - 1, edge(i), pltpu.roll(x, tokens - 1, 0))
            twice = pltpu.roll(x, tokens - 2, 0)
            twice = jnp.where(row == tokens - 1, edge(i + 1), jnp.where(row == tokens - 2, edge(i), twice))
            total = tap(s, 0) * x
            total = total + tap(s, 1) * once
            ref[:, at] = (total + tap(s, 2) * twice).astype(BF16)
        filter_ref[:, at] = grad_filter
        for s in range(3):
            taps_out_ref[s, :, at] = edges[SUMS + 3 * s : SUMS + 3 * s + 3]
        skip_out_ref[:, at] = edges[SUMS + 9 : SUMS + 10]


def per_device(one, two, value, long_filter, short_taps, skip_gain, out_grad):
    devices = lax.axis_size("seq")
    tokens, channels = one.shape
    parts = channels // LANES
    own = LANES // devices
    anywhere = pl.BlockSpec(memory_space=pl.ANY)
    vmem = pl.BlockSpec(memory_space=pltpu.VMEM)
    smem = pl.BlockSpec(memory_space=pltpu.SMEM)
    consts = [jnp.asarray(t) for t in tables(devices, tokens, own)]
    big = (long_filter, two, value, one, out_grad, *consts)
    inward = (parts, devices, 5, own, tokens)
    outward = (parts, devices, 3, own, tokens)
    got, edges = pl.pallas_call(
        functools.partial(exchange_kernel, devices, parts, own),
        out_shape=(
            jax.ShapeDtypeStruct(outward, BF16),
            jax.ShapeDtypeStruct((devices, 1, tokens), F32),
        ),
        in_specs=[anywhere] * len(big) + [smem] * 2,
        out_specs=(anywhere, anywhere),
        scratch_shapes=[pltpu.VMEM(x.shape, x.dtype) for x in big]
        + [
            pltpu.VMEM(inward, BF16),
            pltpu.VMEM(inward, BF16),
            pltpu.VMEM(outward, BF16),
            pltpu.VMEM((devices, 1, tokens), F32),
            pltpu.SemaphoreType.DMA((len(big),)),
            pltpu.SemaphoreType.DMA((parts,)),
            pltpu.SemaphoreType.DMA((parts,)),
            pltpu.SemaphoreType.DMA((parts,)),
            pltpu.SemaphoreType.DMA((parts,)),
            pltpu.SemaphoreType.DMA((2,)),
        ],
        compiler_params=pltpu.CompilerParams(
            collective_id=0, has_side_effects=True, vmem_limit_bytes=56 * 1024 * 1024
        ),
        name="exchange",
    )(*big, short_taps, skip_gain)
    full = jax.ShapeDtypeStruct((tokens, channels), BF16)
    *outs, skip = pl.pallas_call(
        finish_kernel,
        out_shape=(
            full, full, full, full,
            jax.ShapeDtypeStruct((tokens, channels), F32),
            jax.ShapeDtypeStruct(short_taps.shape, F32),
            jax.ShapeDtypeStruct((1, channels), F32),
        ),
        in_specs=[vmem] * 7,
        out_specs=(vmem,) * 7,
        name="finish",
    )(got, edges, one, two, value, out_grad, short_taps)
    return (*outs, skip.reshape(channels))


def solution(mesh):
    rows, lanes = P("seq", "ch"), P("ch")
    taps = P(None, None, "ch")
    return jax.shard_map(
        per_device,
        mesh=mesh,
        in_specs=(rows, rows, rows, rows, taps, lanes, rows),
        out_specs=(rows, rows, rows, rows, rows, taps, lanes),
        check_vma=False,
    )
```

```python
import functools
import math

import jax
import jax.numpy as jnp
import numpy as np
from jax import lax
from jax.experimental import pallas as pl
from jax.experimental.pallas import tpu as pltpu
from jax.sharding import PartitionSpec as P

MESH = pl.DeviceIdType.MESH
F32 = jnp.float32
BF16 = jnp.bfloat16
LANES = 128
ROWS_Z = 16
HALO_LATER, HALO_SOONER, SUMS, FIELD = 0, 6, 12, 32


def halves(table):
    high = table.astype(BF16)
    low = (table - high.astype(np.float64)).astype(BF16)
    return high, low


def tables(devices, tokens, own):
    length = 2 * devices * tokens
    a = np.arange(devices)
    b = np.arange(tokens)
    odd = np.arange(devices) + 0.5
    outer = 2 * math.pi * np.outer(odd, a) / (2 * devices)
    first = np.concatenate([np.cos(outer), -np.sin(outer)], 0)
    last = np.concatenate([np.cos(outer.T), np.sin(outer.T)], 1) * (2.0 / length)
    turn = 2 * math.pi * np.outer(odd, b) / length
    inner = 2 * math.pi * (np.outer(b, b) % tokens) / tokens
    cosine, sine = np.cos(inner), np.sin(inner)
    second = np.block([[cosine, -sine], [sine, cosine]])
    order = np.zeros((own * devices, own * devices))
    for c in range(own):
        order[c * devices + a, a * own + c] = 1.0
    return (
        np.concatenate(halves(first), 0),
        np.stack(halves(last)),
        np.stack([np.cos(turn), -np.sin(turn)]).astype(np.float32),
        np.stack(halves(second)),
        np.stack([order, order.T]).astype(BF16),
    )


def split(x):
    high = x.astype(BF16)
    return high, (x - high.astype(F32)).astype(BF16)


def mul(a, b):
    return jnp.dot(a, b, preferred_element_type=F32)


def exchange_kernel(
    devices, parts, own, rows_z,
    filter_in, two_in, value_in, one_in, cot_in, first_in, last_in, turn_in, second_in, order_in,
    taps_in, skip_in,
    out_ref,
    filter_ref, two_ref, value_ref, one_ref, cot_ref,
    first_ref, last_ref, turn_ref, second_ref, order_ref,
    taps_ref, skip_ref,
    send, recv, ret,
    load_sem, send_sem, recv_sem, ret_sem, out_sem,
):
    me = lax.axis_index("seq")
    tokens = filter_ref.shape[0]
    rows_x = devices // rows_z
    my_x, my_z = me // rows_z, lax.rem(me, rows_z)

    columns = [lax.rem(my_x + dx, rows_x) * rows_z for dx in range(rows_x)]
    middle = rows_z // 2

    def farthest_first(visit):
        def line(dz):
            z = lax.rem(my_z + dz, rows_z)
            for column in columns:
                visit(column + z)

        def both(i, carry):
            line(middle + i)
            line(middle - i)
            return carry

        line(middle)
        lax.fori_loop(1, middle, both, 0)
        for column in columns[1:]:
            visit(column + my_z)

    barrier = pltpu.get_barrier_semaphore()
    farthest_first(
        lambda d: pl.semaphore_signal(barrier, inc=1, device_id={"seq": d}, device_id_type=MESH)
    )

    inputs = (
        filter_in, two_in, value_in, one_in, cot_in,
        first_in, last_in, turn_in, second_in, order_in, taps_in, skip_in,
    )
    held = (
        filter_ref, two_ref, value_ref, one_ref, cot_ref,
        first_ref, last_ref, turn_ref, second_ref, order_ref, taps_ref, skip_ref,
    )
    loads = [pltpu.make_async_copy(x, y, load_sem.at[i]) for i, (x, y) in enumerate(zip(inputs, held))]
    for load in loads:
        load.start()

    def spread(src, dst, at, ssem, rsem):
        def visit(d):
            pltpu.make_async_remote_copy(
                src.at[d, at], dst.at[me, at], ssem, rsem, device_id={"seq": d}, device_id_type=MESH
            ).start()

        farthest_first(visit)
        pltpu.make_async_copy(src.at[me, at], dst.at[me, at], rsem).start()

    others = pl.ds(0, devices - 1)

    def settle(ref, sem):
        pltpu.make_async_copy(ref, ref, sem).wait()

    for p in range(5):
        loads[p].wait()
        for h in range(parts):
            block = held[p][:, h * LANES : (h + 1) * LANES].T
            send[h, :, p] = block.reshape(devices, own, tokens)
    pl.semaphore_wait(barrier, devices - 1)
    inward = ((pl.ds(0, 3), pl.ds(3, 2)),) * parts
    outward = ((pl.ds(0, 3),), (pl.ds(3, 1), pl.ds(4, 3)))
    for h in range(parts):
        for i, at in enumerate(inward[h]):
            spread(send.at[h], recv.at[h], at, send_sem.at[h, i], recv_sem.at[h, i])
    for load in loads[5:]:
        load.wait()

    def sent():
        for h in range(parts):
            for i, at in enumerate(inward[h]):
                settle(send.at[h, others, at], send_sem.at[h, i])

    lane = lax.broadcasted_iota(jnp.int32, (devices, tokens), 1)
    row = lax.broadcasted_iota(jnp.int32, (devices, tokens), 0)

    def later(x, j):
        r = pltpu.roll(x, j, 1)
        up = jnp.where(row == 0, 0.0, pltpu.roll(r, 1, 0))
        return jnp.where(lane < j, up, r)

    def short(s, channel, x):
        moved = (x, later(x, 1), later(x, 2))
        total = taps_ref[s, 0, channel] * moved[0]
        total = total + taps_ref[s, 1, channel] * moved[1]
        return total + taps_ref[s, 2, channel] * moved[2], moved

    turn_re, turn_im = turn_ref[0], turn_ref[1]

    def rotate(re, im):
        return re * turn_re - im * turn_im, re * turn_im + im * turn_re

    def mul_second(x):
        high, low = split(x)
        return mul(high, second_ref[0]) + (mul(low, second_ref[0]) + mul(high, second_ref[1]))

    def rows_of(x, i):
        return x[i * devices : (i + 1) * devices]

    def forward(pieces):
        rows = []
        for x in pieces:
            both = mul(first_ref[...], x)
            both = both[: 2 * devices] + both[2 * devices :]
            rows.append(jnp.concatenate(rotate(both[:devices], both[devices:]), 1))
        full = mul_second(jnp.concatenate(rows, 0))
        size = own * devices
        return [
            (full[i * size : (i + 1) * size, :tokens], full[i * size : (i + 1) * size, tokens:])
            for i in range(len(pieces) // own)
        ]

    def inverse(spectra):
        full = mul_second(jnp.concatenate([jnp.concatenate(z, 1) for z in spectra], 0))
        result = []
        for i in range(len(spectra) * own):
            part = rows_of(full, i)
            high, low = split(jnp.concatenate(rotate(part[:, :tokens], part[:, tokens:]), 0))
            result.append(mul(last_ref[0], high) + (mul(last_ref[0], low) + mul(last_ref[1], high)))
        return [result[i * own : (i + 1) * own] for i in range(len(spectra))]

    ones = jnp.ones((tokens, tokens), BF16)

    def gather(h, p):
        x = mul(order_ref[0], recv[h, :, p].reshape(devices * own, tokens))
        return [rows_of(x, c) for c in range(own)]

    def give(p, pieces):
        stacked = jnp.concatenate([x.astype(BF16) for x in pieces], 0)
        ret[:, p] = mul(order_ref[1], stacked).astype(BF16).reshape(devices, own, tokens)

    each = range(own)
    edges = jnp.zeros((devices, tokens), F32)
    for h in range(parts):
        channels = [h * LANES + own * me + c for c in each]
        skip = [skip_ref[channels[c]] for c in each]
        settle(recv.at[h, :, inward[h][0]], recv_sem.at[h, 0])
        filt = [x.astype(BF16) for x in gather(h, 0)]
        two = [short(1, channels[c], x) for c, x in enumerate(gather(h, 1))]
        val = [short(2, channels[c], x) for c, x in enumerate(gather(h, 2))]
        mixed = [(two[c][0] * val[c][0]).astype(BF16) for c in each]
        (f_re, f_im), (m_re, m_im) = forward(filt + mixed)
        (conv,) = inverse([(m_re * f_re - m_im * f_im, -(m_re * f_im + m_im * f_re))])
        mixed_wide = [x.astype(F32) for x in mixed]
        long_out = [conv[c] + skip[c] * mixed_wide[c] for c in each]
        give(3 * h, long_out)
        if h == parts - 1:
            spread(ret, out_ref, outward[h][0], ret_sem.at[h, 0], out_sem.at[h, 0])

        settle(recv.at[h, :, inward[h][1]], recv_sem.at[h, 1])
        one = [short(0, channels[c], x) for c, x in enumerate(gather(h, 3))]
        cot = gather(h, 4)
        back = [(cot[c] * one[c][0]).astype(BF16) for c in each]
        ((b_re, b_im),) = forward(back)
        grad_mixed, grad_filter = inverse([
            (b_re * f_re + b_im * f_im, b_re * f_im - b_im * f_re),
            (b_re * m_re + b_im * m_im, b_re * m_im - b_im * m_re),
        ])
        back_wide = [x.astype(F32) for x in back]
        grad_in = [grad_mixed[c] + skip[c] * back_wide[c] for c in each]
        give(3 * h + 1, grad_in)
        give(3 * h + 2, grad_filter)
        if h < parts - 1:
            sent()
            spread(ret, out_ref, outward[h][0], ret_sem.at[h, 0], out_sem.at[h, 0])
        sections = []
        for c in each:
            field = FIELD * (own * h + c)
            grads = (cot[c] * long_out[c], grad_in[c] * val[c][0], grad_in[c] * two[c][0])
            streams = (one[c][1], two[c][1], val[c][1])
            for s in range(3):
                at = field + HALO_LATER + 2 * s
                piece = pltpu.roll(streams[s][2], at, 1) if at else streams[s][2]
                edges = jnp.where((lane >= at) & (lane < at + 2), piece, edges)
                at = field + HALO_SOONER + 2 * s
                ahead = jnp.where(row == devices - 1, 0.0, pltpu.roll(grads[s], devices - 1, 0))
                edges = jnp.where((lane >= at) & (lane < at + 2), pltpu.roll(ahead, at, 1), edges)
                for j in range(3):
                    sections.append(grads[s] * streams[s][j])
            sections.append(back_wide[c] * mixed_wide[c])
            sections += [None] * 6
        gathered = [
            jnp.zeros((8, tokens), F32) if x is None else x.reshape(devices // 8, 8, tokens).sum(0)
            for x in sections
        ]
        high, low = split(jnp.concatenate(gathered, 0))
        totals = mul(high, ones) + mul(low, ones)
        section = lax.broadcasted_iota(jnp.int32, totals.shape, 0) // 8
        target = FIELD * (own * h + section // 16) + SUMS + section % 16
        pick = lax.broadcasted_iota(jnp.int32, totals.shape, 1) == target
        edges = edges + jnp.where(pick, totals, 0.0).sum(0, keepdims=True)
    give(3 * parts, split(edges))
    spread(ret, out_ref, outward[-1][1], ret_sem.at[parts - 1, 1], out_sem.at[parts - 1, 1])

    for h in range(parts):
        for i, at in enumerate(outward[h]):
            settle(ret.at[others, at], ret_sem.at[h, i])
            settle(out_ref.at[:, at], out_sem.at[h, i])


def finish_kernel(
    got_ref, one_ref, two_ref, value_ref, cot_ref, taps_ref,
    mixed_out_ref, grad_one_ref, grad_two_ref, grad_value_ref, filter_ref, taps_out_ref, skip_out_ref,
):
    devices, units, own, tokens = got_ref.shape
    parts = units // 3
    source = lax.broadcasted_iota(jnp.int32, (LANES, LANES), 0)
    target = lax.broadcasted_iota(jnp.int32, (LANES, LANES), 1)
    row = lax.broadcasted_iota(jnp.int32, (tokens, LANES), 0)

    def turn(p):
        return got_ref[:, p].reshape(LANES, tokens).T

    turned = turn(3 * parts)
    for h in range(parts):
        at = slice(h * LANES, (h + 1) * LANES)
        long_out, grad_in, grad_filter = [turn(3 * h + p) for p in range(3)]
        long_out, grad_in = long_out.astype(F32), grad_in.astype(F32)
        edges = jnp.zeros((FIELD, LANES), F32)
        for c in range(own):
            place = jnp.where((source // own == target // own) & (target % own == c), 1.0, 0.0)
            field = FIELD * (own * h + c)
            edges = edges + mul(turned[field : field + FIELD], place.astype(BF16))

        def edge(i):
            return edges[i : i + 1]

        def tap(s, j):
            return taps_ref[s, j : j + 1, at]

        gates = []
        for s, ref in enumerate((one_ref, two_ref, value_ref)):
            x = ref[:, at].astype(F32)
            i = HALO_LATER + 2 * s
            once = jnp.where(row == 0, edge(i + 1), pltpu.roll(x, 1, 0))
            twice = jnp.where(row == 0, edge(i), jnp.where(row == 1, edge(i + 1), pltpu.roll(x, 2, 0)))
            total = tap(s, 0) * x
            total = total + tap(s, 1) * once
            gates.append(total + tap(s, 2) * twice)
        mixed_out_ref[:, at] = (gates[0] * long_out).astype(BF16)
        grads = (cot_ref[:, at].astype(F32) * long_out, grad_in * gates[2], grad_in * gates[1])
        for s, ref in enumerate((grad_one_ref, grad_two_ref, grad_value_ref)):
            x = grads[s]
            i = HALO_SOONER + 2 * s
            once = jnp.where(row == tokens - 1, edge(i), pltpu.roll(x, tokens - 1, 0))
            twice = pltpu.roll(x, tokens - 2, 0)
            twice = jnp.where(row == tokens - 1, edge(i + 1), jnp.where(row == tokens - 2, edge(i), twice))
            total = tap(s, 0) * x
            total = total + tap(s, 1) * once
            ref[:, at] = (total + tap(s, 2) * twice).astype(BF16)
        filter_ref[:, at] = grad_filter.astype(F32)
        for s in range(3):
            taps_out_ref[s, :, at] = edges[SUMS + 3 * s : SUMS + 3 * s + 3]
        skip_out_ref[:, at] = edges[SUMS + 9 : SUMS + 10]


def per_device(rows_z, one, two, value, long_filter, short_taps, skip_gain, out_grad):
    devices = lax.axis_size("seq")
    tokens, channels = one.shape
    parts = channels // LANES
    own = LANES // devices
    anywhere = pl.BlockSpec(memory_space=pl.ANY)
    vmem = pl.BlockSpec(memory_space=pltpu.VMEM)
    consts = [jnp.asarray(t) for t in tables(devices, tokens, own)]
    big = (long_filter, two, value, one, out_grad, *consts)
    inward = (parts, devices, 5, own, tokens)
    outward = (devices, 3 * parts + 1, own, tokens)
    got = pl.pallas_call(
        functools.partial(exchange_kernel, devices, parts, own, rows_z),
        out_shape=jax.ShapeDtypeStruct(outward, BF16),
        in_specs=[anywhere] * (len(big) + 2),
        out_specs=anywhere,
        scratch_shapes=[pltpu.VMEM(x.shape, x.dtype) for x in big]
        + [
            pltpu.SMEM(short_taps.shape, F32),
            pltpu.SMEM(skip_gain.shape, F32),
            pltpu.VMEM(inward, BF16),
            pltpu.VMEM(inward, BF16),
            pltpu.VMEM(outward, BF16),
            pltpu.SemaphoreType.DMA((len(big) + 2,)),
            pltpu.SemaphoreType.DMA((parts, 2)),
            pltpu.SemaphoreType.DMA((parts, 2)),
            pltpu.SemaphoreType.DMA((parts, 2)),
            pltpu.SemaphoreType.DMA((parts, 2)),
        ],
        compiler_params=pltpu.CompilerParams(
            collective_id=0, has_side_effects=True, vmem_limit_bytes=56 * 1024 * 1024
        ),
        name="exchange",
    )(*big, short_taps, skip_gain)
    full = jax.ShapeDtypeStruct((tokens, channels), BF16)
    *outs, skip = pl.pallas_call(
        finish_kernel,
        out_shape=(
            full, full, full, full,
            jax.ShapeDtypeStruct((tokens, channels), F32),
            jax.ShapeDtypeStruct(short_taps.shape, F32),
            jax.ShapeDtypeStruct((1, channels), F32),
        ),
        in_specs=[vmem] * 6,
        out_specs=(vmem,) * 7,
        name="finish",
    )(got, one, two, value, out_grad, short_taps)
    return (*outs, skip.reshape(channels))


def solution(mesh):
    rows, lanes = P("seq", "ch"), P("ch")
    taps = P(None, None, "ch")
    return jax.shard_map(
        functools.partial(per_device, ROWS_Z),
        mesh=mesh,
        in_specs=(rows, rows, rows, rows, taps, lanes, rows),
        out_specs=(rows, rows, rows, rows, rows, taps, lanes),
        check_vma=False,
    )
```

```python
import functools
import math

import jax
import jax.numpy as jnp
import numpy as np
from jax import lax
from jax.experimental import pallas as pl
from jax.experimental.pallas import tpu as pltpu
from jax.sharding import PartitionSpec as P

MESH = pl.DeviceIdType.MESH
F32 = jnp.float32
BF16 = jnp.bfloat16
LANES = 128
ROWS_Z = 16
HALO_LATER, HALO_SOONER, SUMS, FIELD = 0, 6, 12, 32


def halves(table):
    high = table.astype(BF16)
    low = (table - high.astype(np.float64)).astype(BF16)
    return high, low


def tables(devices, tokens, own):
    length = 2 * devices * tokens
    a = np.arange(devices)
    b = np.arange(tokens)
    odd = np.arange(devices) + 0.5
    outer = 2 * math.pi * np.outer(odd, a) / (2 * devices)
    first = np.concatenate([np.cos(outer), -np.sin(outer)], 0)
    last = np.concatenate([np.cos(outer.T), np.sin(outer.T)], 1) * (2.0 / length)
    turn = 2 * math.pi * np.outer(odd, b) / length
    inner = 2 * math.pi * (np.outer(b, b) % tokens) / tokens
    cosine, sine = np.cos(inner), np.sin(inner)
    second = np.block([[cosine, -sine], [sine, cosine]])
    order = np.zeros((own * devices, own * devices))
    for c in range(own):
        order[c * devices + a, a * own + c] = 1.0
    return (
        np.concatenate(halves(first), 0),
        np.stack(halves(last)),
        np.stack([np.cos(turn), -np.sin(turn)]).astype(np.float32),
        np.stack(halves(second)),
        np.stack([order, order.T]).astype(BF16),
    )


def split(x):
    high = x.astype(BF16)
    return high, (x - high.astype(F32)).astype(BF16)


def mul(a, b):
    return jnp.dot(a, b, preferred_element_type=F32)


def exchange_kernel(
    devices, parts, own, rows_z,
    filter_in, two_in, value_in, one_in, cot_in, first_in, last_in, turn_in, second_in, order_in,
    taps_in, skip_in,
    out_ref,
    filter_ref, two_ref, value_ref, one_ref, cot_ref,
    first_ref, last_ref, turn_ref, second_ref, order_ref,
    taps_ref, skip_ref,
    send, recv, ret,
    load_sem, send_sem, recv_sem, ret_sem, out_sem,
):
    me = lax.axis_index("seq")
    tokens = filter_ref.shape[0]
    rows_x = devices // rows_z
    my_x, my_z = me // rows_z, lax.rem(me, rows_z)

    columns = [lax.rem(my_x + dx, rows_x) * rows_z for dx in range(rows_x)]
    middle = rows_z // 2

    def farthest_first(visit):
        def line(dz):
            z = lax.rem(my_z + dz, rows_z)
            for column in columns:
                visit(column + z)

        def both(i, carry):
            line(middle + i)
            line(middle - i)
            return carry

        line(middle)
        lax.fori_loop(1, middle, both, 0)
        for column in columns[1:]:
            visit(column + my_z)

    barrier = pltpu.get_barrier_semaphore()
    farthest_first(
        lambda d: pl.semaphore_signal(barrier, inc=1, device_id={"seq": d}, device_id_type=MESH)
    )

    inputs = (
        filter_in, two_in, value_in, one_in, cot_in,
        first_in, last_in, turn_in, second_in, order_in, taps_in, skip_in,
    )
    held = (
        filter_ref, two_ref, value_ref, one_ref, cot_ref,
        first_ref, last_ref, turn_ref, second_ref, order_ref, taps_ref, skip_ref,
    )
    loads = [pltpu.make_async_copy(x, y, load_sem.at[i]) for i, (x, y) in enumerate(zip(inputs, held))]
    for load in loads:
        load.start()

    def spread(src, dst, at, ssem, rsem):
        def visit(d):
            pltpu.make_async_remote_copy(
                src.at[d, at], dst.at[me, at], ssem, rsem, device_id={"seq": d}, device_id_type=MESH
            ).start()

        farthest_first(visit)
        pltpu.make_async_copy(src.at[me, at], dst.at[me, at], rsem).start()

    others = pl.ds(0, devices - 1)

    def settle(ref, sem):
        pltpu.make_async_copy(ref, ref, sem).wait()

    for p in range(5):
        loads[p].wait()
        for h in range(parts):
            block = held[p][:, h * LANES : (h + 1) * LANES].T
            send[h, :, p] = block.reshape(devices, own, tokens)
    pl.semaphore_wait(barrier, devices - 1)
    outward = (pl.ds(0, 3), pl.ds(3, 4))
    for h in range(parts):
        spread(send.at[h], recv.at[h], pl.ds(0, 5), send_sem.at[h], recv_sem.at[h])
    for load in loads[5:]:
        load.wait()

    def sent():
        for h in range(parts):
            settle(send.at[h, others], send_sem.at[h])

    lane = lax.broadcasted_iota(jnp.int32, (devices, tokens), 1)
    row = lax.broadcasted_iota(jnp.int32, (devices, tokens), 0)

    def later(x, j):
        r = pltpu.roll(x, j, 1)
        up = jnp.where(row == 0, 0.0, pltpu.roll(r, 1, 0))
        return jnp.where(lane < j, up, r)

    def short(s, channel, x):
        moved = (x, later(x, 1), later(x, 2))
        total = taps_ref[s, 0, channel] * moved[0]
        total = total + taps_ref[s, 1, channel] * moved[1]
        return total + taps_ref[s, 2, channel] * moved[2], moved

    turn_re, turn_im = turn_ref[0], turn_ref[1]

    def rotate(re, im):
        return re * turn_re - im * turn_im, re * turn_im + im * turn_re

    def mul_second(x):
        high, low = split(x)
        return mul(high, second_ref[0]) + (mul(low, second_ref[0]) + mul(high, second_ref[1]))

    def rows_of(x, i):
        return x[i * devices : (i + 1) * devices]

    def forward(pieces):
        rows = []
        for x in pieces:
            both = mul(first_ref[...], x)
            both = both[: 2 * devices] + both[2 * devices :]
            rows.append(jnp.concatenate(rotate(both[:devices], both[devices:]), 1))
        full = mul_second(jnp.concatenate(rows, 0))
        size = own * devices
        return [
            (full[i * size : (i + 1) * size, :tokens], full[i * size : (i + 1) * size, tokens:])
            for i in range(len(pieces) // own)
        ]

    def inverse(spectra):
        full = mul_second(jnp.concatenate([jnp.concatenate(z, 1) for z in spectra], 0))
        result = []
        for i in range(len(spectra) * own):
            part = rows_of(full, i)
            high, low = split(jnp.concatenate(rotate(part[:, :tokens], part[:, tokens:]), 0))
            result.append(mul(last_ref[0], high) + (mul(last_ref[0], low) + mul(last_ref[1], high)))
        return [result[i * own : (i + 1) * own] for i in range(len(spectra))]

    ones = jnp.ones((tokens, tokens), BF16)

    def gather(h, p):
        x = mul(order_ref[0], recv[h, :, p].reshape(devices * own, tokens))
        return [rows_of(x, c) for c in range(own)]

    def give(p, pieces):
        stacked = jnp.concatenate([x.astype(BF16) for x in pieces], 0)
        ret[:, p] = mul(order_ref[1], stacked).astype(BF16).reshape(devices, own, tokens)

    each = range(own)
    edges = jnp.zeros((devices, tokens), F32)
    for h in range(parts):
        channels = [h * LANES + own * me + c for c in each]
        skip = [skip_ref[channels[c]] for c in each]
        settle(recv.at[h], recv_sem.at[h])
        filt = [x.astype(BF16) for x in gather(h, 0)]
        two = [short(1, channels[c], x) for c, x in enumerate(gather(h, 1))]
        val = [short(2, channels[c], x) for c, x in enumerate(gather(h, 2))]
        one = [short(0, channels[c], x) for c, x in enumerate(gather(h, 3))]
        cot = gather(h, 4)
        mixed = [(two[c][0] * val[c][0]).astype(BF16) for c in each]
        back = [(cot[c] * one[c][0]).astype(BF16) for c in each]
        (f_re, f_im), (m_re, m_im), (b_re, b_im) = forward(filt + mixed + back)
        conv, grad_mixed, grad_filter = inverse([
            (m_re * f_re - m_im * f_im, -(m_re * f_im + m_im * f_re)),
            (b_re * f_re + b_im * f_im, b_re * f_im - b_im * f_re),
            (b_re * m_re + b_im * m_im, b_re * m_im - b_im * m_re),
        ])
        mixed_wide = [x.astype(F32) for x in mixed]
        long_out = [conv[c] + skip[c] * mixed_wide[c] for c in each]
        give(3 * h, long_out)
        back_wide = [x.astype(F32) for x in back]
        grad_in = [grad_mixed[c] + skip[c] * back_wide[c] for c in each]
        give(3 * h + 1, grad_in)
        give(3 * h + 2, grad_filter)
        if h < parts - 1:
            sent()
            spread(ret, out_ref, outward[h], ret_sem.at[h], out_sem.at[h])
        sections = []
        for c in each:
            field = FIELD * (own * h + c)
            grads = (cot[c] * long_out[c], grad_in[c] * val[c][0], grad_in[c] * two[c][0])
            streams = (one[c][1], two[c][1], val[c][1])
            for s in range(3):
                at = field + HALO_LATER + 2 * s
                piece = pltpu.roll(streams[s][2], at, 1) if at else streams[s][2]
                edges = jnp.where((lane >= at) & (lane < at + 2), piece, edges)
                at = field + HALO_SOONER + 2 * s
                ahead = jnp.where(row == devices - 1, 0.0, pltpu.roll(grads[s], devices - 1, 0))
                edges = jnp.where((lane >= at) & (lane < at + 2), pltpu.roll(ahead, at, 1), edges)
                for j in range(3):
                    sections.append(grads[s] * streams[s][j])
            sections.append(back_wide[c] * mixed_wide[c])
            sections += [None] * 6
        gathered = [
            jnp.zeros((8, tokens), F32) if x is None else x.reshape(devices // 8, 8, tokens).sum(0)
            for x in sections
        ]
        high, low = split(jnp.concatenate(gathered, 0))
        totals = mul(high, ones) + mul(low, ones)
        section = lax.broadcasted_iota(jnp.int32, totals.shape, 0) // 8
        target = FIELD * (own * h + section // 16) + SUMS + section % 16
        pick = lax.broadcasted_iota(jnp.int32, totals.shape, 1) == target
        edges = edges + jnp.where(pick, totals, 0.0).sum(0, keepdims=True)
    give(3 * parts, split(edges))
    spread(ret, out_ref, outward[-1], ret_sem.at[parts - 1], out_sem.at[parts - 1])

    for h in range(parts):
        settle(ret.at[others, outward[h]], ret_sem.at[h])
        settle(out_ref.at[:, outward[h]], out_sem.at[h])


def finish_kernel(
    got_ref, one_ref, two_ref, value_ref, cot_ref, taps_ref,
    mixed_out_ref, grad_one_ref, grad_two_ref, grad_value_ref, filter_ref, taps_out_ref, skip_out_ref,
):
    devices, units, own, tokens = got_ref.shape
    parts = units // 3
    source = lax.broadcasted_iota(jnp.int32, (LANES, LANES), 0)
    target = lax.broadcasted_iota(jnp.int32, (LANES, LANES), 1)
    row = lax.broadcasted_iota(jnp.int32, (tokens, LANES), 0)

    def turn(p):
        return got_ref[:, p].reshape(LANES, tokens).T

    turned = turn(3 * parts)
    for h in range(parts):
        at = slice(h * LANES, (h + 1) * LANES)
        long_out, grad_in, grad_filter = [turn(3 * h + p) for p in range(3)]
        long_out, grad_in = long_out.astype(F32), grad_in.astype(F32)
        edges = jnp.zeros((FIELD, LANES), F32)
        for c in range(own):
            place = jnp.where((source // own == target // own) & (target % own == c), 1.0, 0.0)
            field = FIELD * (own * h + c)
            edges = edges + mul(turned[field : field + FIELD], place.astype(BF16))

        def edge(i):
            return edges[i : i + 1]

        def tap(s, j):
            return taps_ref[s, j : j + 1, at]

        gates = []
        for s, ref in enumerate((one_ref, two_ref, value_ref)):
            x = ref[:, at].astype(F32)
            i = HALO_LATER + 2 * s
            once = jnp.where(row == 0, edge(i + 1), pltpu.roll(x, 1, 0))
            twice = jnp.where(row == 0, edge(i), jnp.where(row == 1, edge(i + 1), pltpu.roll(x, 2, 0)))
            total = tap(s, 0) * x
            total = total + tap(s, 1) * once
            gates.append(total + tap(s, 2) * twice)
        mixed_out_ref[:, at] = (gates[0] * long_out).astype(BF16)
        grads = (cot_ref[:, at].astype(F32) * long_out, grad_in * gates[2], grad_in * gates[1])
        for s, ref in enumerate((grad_one_ref, grad_two_ref, grad_value_ref)):
            x = grads[s]
            i = HALO_SOONER + 2 * s
            once = jnp.where(row == tokens - 1, edge(i), pltpu.roll(x, tokens - 1, 0))
            twice = pltpu.roll(x, tokens - 2, 0)
            twice = jnp.where(row == tokens - 1, edge(i + 1), jnp.where(row == tokens - 2, edge(i), twice))
            total = tap(s, 0) * x
            total = total + tap(s, 1) * once
            ref[:, at] = (total + tap(s, 2) * twice).astype(BF16)
        filter_ref[:, at] = grad_filter.astype(F32)
        for s in range(3):
            taps_out_ref[s, :, at] = edges[SUMS + 3 * s : SUMS + 3 * s + 3]
        skip_out_ref[:, at] = edges[SUMS + 9 : SUMS + 10]


def per_device(rows_z, one, two, value, long_filter, short_taps, skip_gain, out_grad):
    devices = lax.axis_size("seq")
    tokens, channels = one.shape
    parts = channels // LANES
    own = LANES // devices
    anywhere = pl.BlockSpec(memory_space=pl.ANY)
    vmem = pl.BlockSpec(memory_space=pltpu.VMEM)
    consts = [jnp.asarray(t) for t in tables(devices, tokens, own)]
    big = (long_filter, two, value, one, out_grad, *consts)
    inward = (parts, devices, 5, own, tokens)
    outward = (devices, 3 * parts + 1, own, tokens)
    got = pl.pallas_call(
        functools.partial(exchange_kernel, devices, parts, own, rows_z),
        out_shape=jax.ShapeDtypeStruct(outward, BF16),
        in_specs=[anywhere] * (len(big) + 2),
        out_specs=anywhere,
        scratch_shapes=[pltpu.VMEM(x.shape, x.dtype) for x in big]
        + [
            pltpu.SMEM(short_taps.shape, F32),
            pltpu.SMEM(skip_gain.shape, F32),
            pltpu.VMEM(inward, BF16),
            pltpu.VMEM(inward, BF16),
            pltpu.VMEM(outward, BF16),
            pltpu.SemaphoreType.DMA((len(big) + 2,)),
            pltpu.SemaphoreType.DMA((parts,)),
            pltpu.SemaphoreType.DMA((parts,)),
            pltpu.SemaphoreType.DMA((parts,)),
            pltpu.SemaphoreType.DMA((parts,)),
        ],
        compiler_params=pltpu.CompilerParams(
            collective_id=0, has_side_effects=True, vmem_limit_bytes=56 * 1024 * 1024
        ),
        name="exchange",
    )(*big, short_taps, skip_gain)
    full = jax.ShapeDtypeStruct((tokens, channels), BF16)
    *outs, skip = pl.pallas_call(
        finish_kernel,
        out_shape=(
            full, full, full, full,
            jax.ShapeDtypeStruct((tokens, channels), F32),
            jax.ShapeDtypeStruct(short_taps.shape, F32),
            jax.ShapeDtypeStruct((1, channels), F32),
        ),
        in_specs=[vmem] * 6,
        out_specs=(vmem,) * 7,
        name="finish",
    )(got, one, two, value, out_grad, short_taps)
    return (*outs, skip.reshape(channels))


def solution(mesh):
    rows, lanes = P("seq", "ch"), P("ch")
    taps = P(None, None, "ch")
    return jax.shard_map(
        functools.partial(per_device, ROWS_Z),
        mesh=mesh,
        in_specs=(rows, rows, rows, rows, taps, lanes, rows),
        out_specs=(rows, rows, rows, rows, rows, taps, lanes),
        check_vma=False,
    )
```

```python
import functools
import math

import jax
import jax.numpy as jnp
import numpy as np
from jax import lax
from jax.experimental import pallas as pl
from jax.experimental.pallas import tpu as pltpu
from jax.sharding import PartitionSpec as P

MESH = pl.DeviceIdType.MESH
F32 = jnp.float32
BF16 = jnp.bfloat16
LANES = 128
ROWS_Z = 16
HALO_LATER, HALO_SOONER, SUMS, FIELD = 0, 6, 12, 32


def halves(table):
    high = table.astype(BF16)
    low = (table - high.astype(np.float64)).astype(BF16)
    return high, low


def tables(devices, tokens, own):
    length = 2 * devices * tokens
    a = np.arange(devices)
    b = np.arange(tokens)
    odd = np.arange(devices) + 0.5
    outer = 2 * math.pi * np.outer(odd, a) / (2 * devices)
    first = np.concatenate([np.cos(outer), -np.sin(outer)], 0)
    last = np.concatenate([np.cos(outer.T), np.sin(outer.T)], 1) * (2.0 / length)
    turn = 2 * math.pi * np.outer(odd, b) / length
    inner = 2 * math.pi * (np.outer(b, b) % tokens) / tokens
    cosine, sine = np.cos(inner), np.sin(inner)
    second = np.block([[cosine, -sine], [sine, cosine]])
    order = np.zeros((own * devices, own * devices))
    for c in range(own):
        order[c * devices + a, a * own + c] = 1.0
    return (
        np.concatenate(halves(first), 0),
        np.stack(halves(last)),
        np.stack([np.cos(turn), -np.sin(turn)]).astype(np.float32),
        np.stack(halves(second)),
        np.stack([order, order.T]).astype(BF16),
    )


def split(x):
    high = x.astype(BF16)
    return high, (x - high.astype(F32)).astype(BF16)


def mul(a, b):
    return jnp.dot(a, b, preferred_element_type=F32)


def exchange_kernel(
    devices, parts, own, rows_z,
    filter_in, two_in, value_in, one_in, cot_in, first_in, last_in, turn_in, second_in, order_in,
    taps_in, skip_in,
    out_ref,
    filter_ref, two_ref, value_ref, one_ref, cot_ref,
    first_ref, last_ref, turn_ref, second_ref, order_ref,
    taps_ref, skip_ref,
    send, recv, ret,
    load_sem, send_sem, recv_sem, ret_sem, out_sem,
):
    me = lax.axis_index("seq")
    tokens = filter_ref.shape[0]
    rows_x = devices // rows_z
    my_x, my_z = me // rows_z, lax.rem(me, rows_z)

    columns = [lax.rem(my_x + dx, rows_x) * rows_z for dx in (2, 1, 3, 0)]
    middle = rows_z // 2

    def farthest_first(visit):
        def line(dz):
            z = lax.rem(my_z + dz, rows_z)
            for column in columns:
                visit(column + z)

        def both(i, carry):
            line(middle + i)
            line(middle - i)
            return carry

        line(middle)
        lax.fori_loop(1, middle, both, 0)
        for column in columns[:-1]:
            visit(column + my_z)

    barrier = pltpu.get_barrier_semaphore()
    farthest_first(
        lambda d: pl.semaphore_signal(barrier, inc=1, device_id={"seq": d}, device_id_type=MESH)
    )

    inputs = (
        filter_in, two_in, value_in, one_in, cot_in,
        first_in, last_in, turn_in, second_in, order_in, taps_in, skip_in,
    )
    held = (
        filter_ref, two_ref, value_ref, one_ref, cot_ref,
        first_ref, last_ref, turn_ref, second_ref, order_ref, taps_ref, skip_ref,
    )
    loads = [pltpu.make_async_copy(x, y, load_sem.at[i]) for i, (x, y) in enumerate(zip(inputs, held))]
    for load in loads:
        load.start()

    def spread(src, dst, at, ssem, rsem):
        def visit(d):
            pltpu.make_async_remote_copy(
                src.at[d, at], dst.at[me, at], ssem, rsem, device_id={"seq": d}, device_id_type=MESH
            ).start()

        farthest_first(visit)
        pltpu.make_async_copy(src.at[me, at], dst.at[me, at], rsem).start()

    others = pl.ds(0, devices - 1)

    def settle(ref, sem):
        pltpu.make_async_copy(ref, ref, sem).wait()

    for p in range(5):
        loads[p].wait()
        for h in range(parts):
            block = held[p][:, h * LANES : (h + 1) * LANES].T
            send[h, :, p] = block.reshape(devices, own, tokens)
    pl.semaphore_wait(barrier, devices - 1)
    outward = (pl.ds(0, 3), pl.ds(3, 4))
    for h in range(parts):
        spread(send.at[h], recv.at[h], pl.ds(0, 5), send_sem.at[h], recv_sem.at[h])
    for load in loads[5:]:
        load.wait()

    def sent():
        for h in range(parts):
            settle(send.at[h, others], send_sem.at[h])

    lane = lax.broadcasted_iota(jnp.int32, (devices, tokens), 1)
    row = lax.broadcasted_iota(jnp.int32, (devices, tokens), 0)

    def later(x, j):
        r = pltpu.roll(x, j, 1)
        up = jnp.where(row == 0, 0.0, pltpu.roll(r, 1, 0))
        return jnp.where(lane < j, up, r)

    def short(s, channel, x):
        moved = (x, later(x, 1), later(x, 2))
        total = taps_ref[s, 0, channel] * moved[0]
        total = total + taps_ref[s, 1, channel] * moved[1]
        return total + taps_ref[s, 2, channel] * moved[2], moved

    turn_re, turn_im = turn_ref[0], turn_ref[1]

    def rotate(re, im):
        return re * turn_re - im * turn_im, re * turn_im + im * turn_re

    def mul_second(x):
        high, low = split(x)
        return mul(high, second_ref[0]) + (mul(low, second_ref[0]) + mul(high, second_ref[1]))

    def rows_of(x, i):
        return x[i * devices : (i + 1) * devices]

    def forward(pieces):
        rows = []
        for x in pieces:
            both = mul(first_ref[...], x)
            both = both[: 2 * devices] + both[2 * devices :]
            rows.append(jnp.concatenate(rotate(both[:devices], both[devices:]), 1))
        full = mul_second(jnp.concatenate(rows, 0))
        size = own * devices
        return [
            (full[i * size : (i + 1) * size, :tokens], full[i * size : (i + 1) * size, tokens:])
            for i in range(len(pieces) // own)
        ]

    def inverse(spectra):
        full = mul_second(jnp.concatenate([jnp.concatenate(z, 1) for z in spectra], 0))
        result = []
        for i in range(len(spectra) * own):
            part = rows_of(full, i)
            high, low = split(jnp.concatenate(rotate(part[:, :tokens], part[:, tokens:]), 0))
            result.append(mul(last_ref[0], high) + (mul(last_ref[0], low) + mul(last_ref[1], high)))
        return [result[i * own : (i + 1) * own] for i in range(len(spectra))]

    ones = jnp.ones((tokens, tokens), BF16)

    def gather(h, p):
        x = mul(order_ref[0], recv[h, :, p].reshape(devices * own, tokens))
        return [rows_of(x, c) for c in range(own)]

    def give(p, pieces):
        stacked = jnp.concatenate([x.astype(BF16) for x in pieces], 0)
        ret[:, p] = mul(order_ref[1], stacked).astype(BF16).reshape(devices, own, tokens)

    each = range(own)
    edges = jnp.zeros((devices, tokens), F32)
    for h in range(parts):
        channels = [h * LANES + own * me + c for c in each]
        skip = [skip_ref[channels[c]] for c in each]
        settle(recv.at[h], recv_sem.at[h])
        filt = [x.astype(BF16) for x in gather(h, 0)]
        two = [short(1, channels[c], x) for c, x in enumerate(gather(h, 1))]
        val = [short(2, channels[c], x) for c, x in enumerate(gather(h, 2))]
        one = [short(0, channels[c], x) for c, x in enumerate(gather(h, 3))]
        cot = gather(h, 4)
        mixed = [(two[c][0] * val[c][0]).astype(BF16) for c in each]
        back = [(cot[c] * one[c][0]).astype(BF16) for c in each]
        (f_re, f_im), (m_re, m_im), (b_re, b_im) = forward(filt + mixed + back)
        conv, grad_mixed, grad_filter = inverse([
            (m_re * f_re - m_im * f_im, -(m_re * f_im + m_im * f_re)),
            (b_re * f_re + b_im * f_im, b_re * f_im - b_im * f_re),
            (b_re * m_re + b_im * m_im, b_re * m_im - b_im * m_re),
        ])
        mixed_wide = [x.astype(F32) for x in mixed]
        long_out = [conv[c] + skip[c] * mixed_wide[c] for c in each]
        give(3 * h, long_out)
        back_wide = [x.astype(F32) for x in back]
        grad_in = [grad_mixed[c] + skip[c] * back_wide[c] for c in each]
        give(3 * h + 1, grad_in)
        give(3 * h + 2, grad_filter)
        if h < parts - 1:
            sent()
            spread(ret, out_ref, outward[h], ret_sem.at[h], out_sem.at[h])
        sections = []
        for c in each:
            field = FIELD * (own * h + c)
            grads = (cot[c] * long_out[c], grad_in[c] * val[c][0], grad_in[c] * two[c][0])
            streams = (one[c][1], two[c][1], val[c][1])
            for s in range(3):
                at = field + HALO_LATER + 2 * s
                piece = pltpu.roll(streams[s][2], at, 1) if at else streams[s][2]
                edges = jnp.where((lane >= at) & (lane < at + 2), piece, edges)
                at = field + HALO_SOONER + 2 * s
                ahead = jnp.where(row == devices - 1, 0.0, pltpu.roll(grads[s], devices - 1, 0))
                edges = jnp.where((lane >= at) & (lane < at + 2), pltpu.roll(ahead, at, 1), edges)
                for j in range(3):
                    sections.append(grads[s] * streams[s][j])
            sections.append(back_wide[c] * mixed_wide[c])
            sections += [None] * 6
        gathered = [
            jnp.zeros((8, tokens), F32) if x is None else x.reshape(devices // 8, 8, tokens).sum(0)
            for x in sections
        ]
        high, low = split(jnp.concatenate(gathered, 0))
        totals = mul(high, ones) + mul(low, ones)
        section = lax.broadcasted_iota(jnp.int32, totals.shape, 0) // 8
        target = FIELD * (own * h + section // 16) + SUMS + section % 16
        pick = lax.broadcasted_iota(jnp.int32, totals.shape, 1) == target
        edges = edges + jnp.where(pick, totals, 0.0).sum(0, keepdims=True)
    give(3 * parts, split(edges))
    spread(ret, out_ref, outward[-1], ret_sem.at[parts - 1], out_sem.at[parts - 1])

    for h in range(parts):
        settle(ret.at[others, outward[h]], ret_sem.at[h])
        settle(out_ref.at[:, outward[h]], out_sem.at[h])


def finish_kernel(
    got_ref, one_ref, two_ref, value_ref, cot_ref, taps_ref,
    mixed_out_ref, grad_one_ref, grad_two_ref, grad_value_ref, filter_ref, taps_out_ref, skip_out_ref,
):
    devices, units, own, tokens = got_ref.shape
    parts = units // 3
    source = lax.broadcasted_iota(jnp.int32, (LANES, LANES), 0)
    target = lax.broadcasted_iota(jnp.int32, (LANES, LANES), 1)
    row = lax.broadcasted_iota(jnp.int32, (tokens, LANES), 0)

    def turn(p):
        return got_ref[:, p].reshape(LANES, tokens).T

    turned = turn(3 * parts)
    for h in range(parts):
        at = slice(h * LANES, (h + 1) * LANES)
        long_out, grad_in, grad_filter = [turn(3 * h + p) for p in range(3)]
        long_out, grad_in = long_out.astype(F32), grad_in.astype(F32)
        edges = jnp.zeros((FIELD, LANES), F32)
        for c in range(own):
            place = jnp.where((source // own == target // own) & (target % own == c), 1.0, 0.0)
            field = FIELD * (own * h + c)
            edges = edges + mul(turned[field : field + FIELD], place.astype(BF16))

        def edge(i):
            return edges[i : i + 1]

        def tap(s, j):
            return taps_ref[s, j : j + 1, at]

        gates = []
        for s, ref in enumerate((one_ref, two_ref, value_ref)):
            x = ref[:, at].astype(F32)
            i = HALO_LATER + 2 * s
            once = jnp.where(row == 0, edge(i + 1), pltpu.roll(x, 1, 0))
            twice = jnp.where(row == 0, edge(i), jnp.where(row == 1, edge(i + 1), pltpu.roll(x, 2, 0)))
            total = tap(s, 0) * x
            total = total + tap(s, 1) * once
            gates.append(total + tap(s, 2) * twice)
        mixed_out_ref[:, at] = (gates[0] * long_out).astype(BF16)
        grads = (cot_ref[:, at].astype(F32) * long_out, grad_in * gates[2], grad_in * gates[1])
        for s, ref in enumerate((grad_one_ref, grad_two_ref, grad_value_ref)):
            x = grads[s]
            i = HALO_SOONER + 2 * s
            once = jnp.where(row == tokens - 1, edge(i), pltpu.roll(x, tokens - 1, 0))
            twice = pltpu.roll(x, tokens - 2, 0)
            twice = jnp.where(row == tokens - 1, edge(i + 1), jnp.where(row == tokens - 2, edge(i), twice))
            total = tap(s, 0) * x
            total = total + tap(s, 1) * once
            ref[:, at] = (total + tap(s, 2) * twice).astype(BF16)
        filter_ref[:, at] = grad_filter.astype(F32)
        for s in range(3):
            taps_out_ref[s, :, at] = edges[SUMS + 3 * s : SUMS + 3 * s + 3]
        skip_out_ref[:, at] = edges[SUMS + 9 : SUMS + 10]


def per_device(rows_z, one, two, value, long_filter, short_taps, skip_gain, out_grad):
    devices = lax.axis_size("seq")
    tokens, channels = one.shape
    parts = channels // LANES
    own = LANES // devices
    anywhere = pl.BlockSpec(memory_space=pl.ANY)
    vmem = pl.BlockSpec(memory_space=pltpu.VMEM)
    consts = [jnp.asarray(t) for t in tables(devices, tokens, own)]
    big = (long_filter, two, value, one, out_grad, *consts)
    inward = (parts, devices, 5, own, tokens)
    outward = (devices, 3 * parts + 1, own, tokens)
    got = pl.pallas_call(
        functools.partial(exchange_kernel, devices, parts, own, rows_z),
        out_shape=jax.ShapeDtypeStruct(outward, BF16),
        in_specs=[anywhere] * (len(big) + 2),
        out_specs=anywhere,
        scratch_shapes=[pltpu.VMEM(x.shape, x.dtype) for x in big]
        + [
            pltpu.SMEM(short_taps.shape, F32),
            pltpu.SMEM(skip_gain.shape, F32),
            pltpu.VMEM(inward, BF16),
            pltpu.VMEM(inward, BF16),
            pltpu.VMEM(outward, BF16),
            pltpu.SemaphoreType.DMA((len(big) + 2,)),
            pltpu.SemaphoreType.DMA((parts,)),
            pltpu.SemaphoreType.DMA((parts,)),
            pltpu.SemaphoreType.DMA((parts,)),
            pltpu.SemaphoreType.DMA((parts,)),
        ],
        compiler_params=pltpu.CompilerParams(
            collective_id=0, has_side_effects=True, vmem_limit_bytes=56 * 1024 * 1024
        ),
        name="exchange",
    )(*big, short_taps, skip_gain)
    full = jax.ShapeDtypeStruct((tokens, channels), BF16)
    *outs, skip = pl.pallas_call(
        finish_kernel,
        out_shape=(
            full, full, full, full,
            jax.ShapeDtypeStruct((tokens, channels), F32),
            jax.ShapeDtypeStruct(short_taps.shape, F32),
            jax.ShapeDtypeStruct((1, channels), F32),
        ),
        in_specs=[vmem] * 6,
        out_specs=(vmem,) * 7,
        name="finish",
    )(got, one, two, value, out_grad, short_taps)
    return (*outs, skip.reshape(channels))


def solution(mesh):
    rows, lanes = P("seq", "ch"), P("ch")
    taps = P(None, None, "ch")
    return jax.shard_map(
        functools.partial(per_device, ROWS_Z),
        mesh=mesh,
        in_specs=(rows, rows, rows, rows, taps, lanes, rows),
        out_specs=(rows, rows, rows, rows, rows, taps, lanes),
        check_vma=False,
    )
```

```python
import functools
import math

import jax
import jax.numpy as jnp
import numpy as np
from jax import lax
from jax.experimental import pallas as pl
from jax.experimental.pallas import tpu as pltpu
from jax.sharding import PartitionSpec as P

MESH = pl.DeviceIdType.MESH
F32 = jnp.float32
BF16 = jnp.bfloat16
LANES = 128
ROWS_Z = 16
HALO_LATER, HALO_SOONER, SUMS, FIELD = 0, 6, 12, 32


def halves(table):
    high = table.astype(BF16)
    low = (table - high.astype(np.float64)).astype(BF16)
    return high, low


def tables(devices, tokens, own):
    length = 2 * devices * tokens
    a = np.arange(devices)
    b = np.arange(tokens)
    odd = np.arange(devices) + 0.5
    outer = 2 * math.pi * np.outer(odd, a) / (2 * devices)
    first = np.concatenate([np.cos(outer), -np.sin(outer)], 0)
    last = np.concatenate([np.cos(outer.T), np.sin(outer.T)], 1) * (2.0 / length)
    turn = 2 * math.pi * np.outer(odd, b) / length
    inner = 2 * math.pi * (np.outer(b, b) % tokens) / tokens
    cosine, sine = np.cos(inner), np.sin(inner)
    second = np.block([[cosine, -sine], [sine, cosine]])
    order = np.zeros((own * devices, own * devices))
    for c in range(own):
        order[c * devices + a, a * own + c] = 1.0
    return (
        np.concatenate(halves(first), 0),
        np.stack(halves(last)),
        np.stack([np.cos(turn), -np.sin(turn)]).astype(np.float32),
        np.stack(halves(second)),
        np.stack([order, order.T]).astype(BF16),
    )


def split(x):
    high = x.astype(BF16)
    return high, (x - high.astype(F32)).astype(BF16)


def mul(a, b):
    return jnp.dot(a, b, preferred_element_type=F32)


def exchange_kernel(
    devices, parts, own, rows_z,
    filter_in, two_in, value_in, one_in, cot_in, first_in, last_in, turn_in, second_in, order_in,
    taps_in, skip_in,
    out_ref,
    filter_ref, two_ref, value_ref, one_ref, cot_ref,
    first_ref, last_ref, turn_ref, second_ref, order_ref,
    taps_ref, skip_ref,
    send, recv, ret,
    load_sem, send_sem, recv_sem, ret_sem, out_sem,
):
    me = lax.axis_index("seq")
    tokens = filter_ref.shape[0]
    rows_x = devices // rows_z
    my_x, my_z = me // rows_z, lax.rem(me, rows_z)

    columns = [lax.rem(my_x + dx, rows_x) * rows_z for dx in (2, 1, 3, 0)]
    middle = rows_z // 2

    def farthest_first(visit):
        def line(dz):
            z = lax.rem(my_z + dz, rows_z)
            for column in columns:
                visit(column + z)

        def both(i, carry):
            line(middle + i)
            line(middle - i)
            return carry

        line(middle)
        lax.fori_loop(1, middle, both, 0)
        for column in columns[:-1]:
            visit(column + my_z)

    barrier = pltpu.get_barrier_semaphore()
    farthest_first(
        lambda d: pl.semaphore_signal(barrier, inc=1, device_id={"seq": d}, device_id_type=MESH)
    )

    inputs = (
        filter_in, two_in, value_in, one_in, cot_in,
        first_in, last_in, turn_in, second_in, order_in, taps_in, skip_in,
    )
    held = (
        filter_ref, two_ref, value_ref, one_ref, cot_ref,
        first_ref, last_ref, turn_ref, second_ref, order_ref, taps_ref, skip_ref,
    )
    loads = [pltpu.make_async_copy(x, y, load_sem.at[i]) for i, (x, y) in enumerate(zip(inputs, held))]
    for load in loads:
        load.start()

    def spread(src, dst, at, ssem, rsem):
        def visit(d):
            pltpu.make_async_remote_copy(
                src.at[d, at], dst.at[me, at], ssem, rsem, device_id={"seq": d}, device_id_type=MESH
            ).start()

        farthest_first(visit)
        pltpu.make_async_copy(src.at[me, at], dst.at[me, at], rsem).start()

    others = pl.ds(0, devices - 1)

    def settle(ref, sem):
        pltpu.make_async_copy(ref, ref, sem).wait()

    for p in range(5):
        loads[p].wait()
        for h in range(parts):
            block = held[p][:, h * LANES : (h + 1) * LANES].T
            send[:, 5 * h + p] = block.reshape(devices, own, tokens)
    pl.semaphore_wait(barrier, devices - 1)
    forth = (pl.ds(0, 6), pl.ds(6, 4))
    outward = (pl.ds(0, 3), pl.ds(3, 4))
    for h in range(parts):
        spread(send, recv, forth[h], send_sem.at[h], recv_sem.at[h])
    for load in loads[5:]:
        load.wait()

    def sent():
        for h in range(parts):
            settle(send.at[others, forth[h]], send_sem.at[h])

    lane = lax.broadcasted_iota(jnp.int32, (devices, tokens), 1)
    row = lax.broadcasted_iota(jnp.int32, (devices, tokens), 0)

    def later(x, j):
        r = pltpu.roll(x, j, 1)
        up = jnp.where(row == 0, 0.0, pltpu.roll(r, 1, 0))
        return jnp.where(lane < j, up, r)

    def short(s, channel, x):
        moved = (x, later(x, 1), later(x, 2))
        total = taps_ref[s, 0, channel] * moved[0]
        total = total + taps_ref[s, 1, channel] * moved[1]
        return total + taps_ref[s, 2, channel] * moved[2], moved

    turn_re, turn_im = turn_ref[0], turn_ref[1]

    def rotate(re, im):
        return re * turn_re - im * turn_im, re * turn_im + im * turn_re

    def mul_second(x):
        high, low = split(x)
        return mul(high, second_ref[0]) + (mul(low, second_ref[0]) + mul(high, second_ref[1]))

    def rows_of(x, i):
        return x[i * devices : (i + 1) * devices]

    def forward(pieces):
        rows = []
        for x in pieces:
            both = mul(first_ref[...], x)
            both = both[: 2 * devices] + both[2 * devices :]
            rows.append(jnp.concatenate(rotate(both[:devices], both[devices:]), 1))
        full = mul_second(jnp.concatenate(rows, 0))
        size = own * devices
        return [
            (full[i * size : (i + 1) * size, :tokens], full[i * size : (i + 1) * size, tokens:])
            for i in range(len(pieces) // own)
        ]

    def inverse(spectra):
        full = mul_second(jnp.concatenate([jnp.concatenate(z, 1) for z in spectra], 0))
        result = []
        for i in range(len(spectra) * own):
            part = rows_of(full, i)
            high, low = split(jnp.concatenate(rotate(part[:, :tokens], part[:, tokens:]), 0))
            result.append(mul(last_ref[0], high) + (mul(last_ref[0], low) + mul(last_ref[1], high)))
        return [result[i * own : (i + 1) * own] for i in range(len(spectra))]

    ones = jnp.ones((tokens, tokens), BF16)

    def gather(h, p):
        x = mul(order_ref[0], recv[:, 5 * h + p].reshape(devices * own, tokens))
        return [rows_of(x, c) for c in range(own)]

    def give(p, pieces):
        stacked = jnp.concatenate([x.astype(BF16) for x in pieces], 0)
        ret[:, p] = mul(order_ref[1], stacked).astype(BF16).reshape(devices, own, tokens)

    each = range(own)
    filters = []
    edges = jnp.zeros((devices, tokens), F32)
    for h in range(parts):
        channels = [h * LANES + own * me + c for c in each]
        skip = [skip_ref[channels[c]] for c in each]
        settle(recv.at[:, forth[h]], recv_sem.at[h])
        fresh = [x.astype(BF16) for k in ((0, 1) if h == 0 else ()) for x in gather(k, 0)]
        two = [short(1, channels[c], x) for c, x in enumerate(gather(h, 1))]
        val = [short(2, channels[c], x) for c, x in enumerate(gather(h, 2))]
        one = [short(0, channels[c], x) for c, x in enumerate(gather(h, 3))]
        cot = gather(h, 4)
        mixed = [(two[c][0] * val[c][0]).astype(BF16) for c in each]
        back = [(cot[c] * one[c][0]).astype(BF16) for c in each]
        (m_re, m_im), (b_re, b_im), *more = forward(mixed + back + fresh)
        filters += more
        f_re, f_im = filters[h]
        conv, grad_mixed, grad_filter = inverse([
            (m_re * f_re - m_im * f_im, -(m_re * f_im + m_im * f_re)),
            (b_re * f_re + b_im * f_im, b_re * f_im - b_im * f_re),
            (b_re * m_re + b_im * m_im, b_re * m_im - b_im * m_re),
        ])
        mixed_wide = [x.astype(F32) for x in mixed]
        long_out = [conv[c] + skip[c] * mixed_wide[c] for c in each]
        give(3 * h, long_out)
        back_wide = [x.astype(F32) for x in back]
        grad_in = [grad_mixed[c] + skip[c] * back_wide[c] for c in each]
        give(3 * h + 1, grad_in)
        give(3 * h + 2, grad_filter)
        if h < parts - 1:
            sent()
            spread(ret, out_ref, outward[h], ret_sem.at[h], out_sem.at[h])
        sections = []
        for c in each:
            field = FIELD * (own * h + c)
            grads = (cot[c] * long_out[c], grad_in[c] * val[c][0], grad_in[c] * two[c][0])
            streams = (one[c][1], two[c][1], val[c][1])
            for s in range(3):
                at = field + HALO_LATER + 2 * s
                piece = pltpu.roll(streams[s][2], at, 1) if at else streams[s][2]
                edges = jnp.where((lane >= at) & (lane < at + 2), piece, edges)
                at = field + HALO_SOONER + 2 * s
                ahead = jnp.where(row == devices - 1, 0.0, pltpu.roll(grads[s], devices - 1, 0))
                edges = jnp.where((lane >= at) & (lane < at + 2), pltpu.roll(ahead, at, 1), edges)
                for j in range(3):
                    sections.append(grads[s] * streams[s][j])
            sections.append(back_wide[c] * mixed_wide[c])
            sections += [None] * 6
        gathered = [
            jnp.zeros((8, tokens), F32) if x is None else x.reshape(devices // 8, 8, tokens).sum(0)
            for x in sections
        ]
        high, low = split(jnp.concatenate(gathered, 0))
        totals = mul(high, ones) + mul(low, ones)
        section = lax.broadcasted_iota(jnp.int32, totals.shape, 0) // 8
        target = FIELD * (own * h + section // 16) + SUMS + section % 16
        pick = lax.broadcasted_iota(jnp.int32, totals.shape, 1) == target
        edges = edges + jnp.where(pick, totals, 0.0).sum(0, keepdims=True)
    give(3 * parts, split(edges))
    spread(ret, out_ref, outward[-1], ret_sem.at[parts - 1], out_sem.at[parts - 1])

    for h in range(parts):
        settle(ret.at[others, outward[h]], ret_sem.at[h])
        settle(out_ref.at[:, outward[h]], out_sem.at[h])


def finish_kernel(
    got_ref, one_ref, two_ref, value_ref, cot_ref, taps_ref,
    mixed_out_ref, grad_one_ref, grad_two_ref, grad_value_ref, filter_ref, taps_out_ref, skip_out_ref,
):
    devices, units, own, tokens = got_ref.shape
    parts = units // 3
    source = lax.broadcasted_iota(jnp.int32, (LANES, LANES), 0)
    target = lax.broadcasted_iota(jnp.int32, (LANES, LANES), 1)
    row = lax.broadcasted_iota(jnp.int32, (tokens, LANES), 0)

    def turn(p):
        return got_ref[:, p].reshape(LANES, tokens).T

    turned = turn(3 * parts)
    for h in range(parts):
        at = slice(h * LANES, (h + 1) * LANES)
        long_out, grad_in, grad_filter = [turn(3 * h + p) for p in range(3)]
        long_out, grad_in = long_out.astype(F32), grad_in.astype(F32)
        edges = jnp.zeros((FIELD, LANES), F32)
        for c in range(own):
            place = jnp.where((source // own == target // own) & (target % own == c), 1.0, 0.0)
            field = FIELD * (own * h + c)
            edges = edges + mul(turned[field : field + FIELD], place.astype(BF16))

        def edge(i):
            return edges[i : i + 1]

        def tap(s, j):
            return taps_ref[s, j : j + 1, at]

        gates = []
        for s, ref in enumerate((one_ref, two_ref, value_ref)):
            x = ref[:, at].astype(F32)
            i = HALO_LATER + 2 * s
            once = jnp.where(row == 0, edge(i + 1), pltpu.roll(x, 1, 0))
            twice = jnp.where(row == 0, edge(i), jnp.where(row == 1, edge(i + 1), pltpu.roll(x, 2, 0)))
            total = tap(s, 0) * x
            total = total + tap(s, 1) * once
            gates.append(total + tap(s, 2) * twice)
        mixed_out_ref[:, at] = (gates[0] * long_out).astype(BF16)
        grads = (cot_ref[:, at].astype(F32) * long_out, grad_in * gates[2], grad_in * gates[1])
        for s, ref in enumerate((grad_one_ref, grad_two_ref, grad_value_ref)):
            x = grads[s]
            i = HALO_SOONER + 2 * s
            once = jnp.where(row == tokens - 1, edge(i), pltpu.roll(x, tokens - 1, 0))
            twice = pltpu.roll(x, tokens - 2, 0)
            twice = jnp.where(row == tokens - 1, edge(i + 1), jnp.where(row == tokens - 2, edge(i), twice))
            total = tap(s, 0) * x
            total = total + tap(s, 1) * once
            ref[:, at] = (total + tap(s, 2) * twice).astype(BF16)
        filter_ref[:, at] = grad_filter.astype(F32)
        for s in range(3):
            taps_out_ref[s, :, at] = edges[SUMS + 3 * s : SUMS + 3 * s + 3]
        skip_out_ref[:, at] = edges[SUMS + 9 : SUMS + 10]


def per_device(rows_z, one, two, value, long_filter, short_taps, skip_gain, out_grad):
    devices = lax.axis_size("seq")
    tokens, channels = one.shape
    parts = channels // LANES
    own = LANES // devices
    anywhere = pl.BlockSpec(memory_space=pl.ANY)
    vmem = pl.BlockSpec(memory_space=pltpu.VMEM)
    consts = [jnp.asarray(t) for t in tables(devices, tokens, own)]
    big = (long_filter, two, value, one, out_grad, *consts)
    inward = (devices, 5 * parts, own, tokens)
    outward = (devices, 3 * parts + 1, own, tokens)
    got = pl.pallas_call(
        functools.partial(exchange_kernel, devices, parts, own, rows_z),
        out_shape=jax.ShapeDtypeStruct(outward, BF16),
        in_specs=[anywhere] * (len(big) + 2),
        out_specs=anywhere,
        scratch_shapes=[pltpu.VMEM(x.shape, x.dtype) for x in big]
        + [
            pltpu.SMEM(short_taps.shape, F32),
            pltpu.SMEM(skip_gain.shape, F32),
            pltpu.VMEM(inward, BF16),
            pltpu.VMEM(inward, BF16),
            pltpu.VMEM(outward, BF16),
            pltpu.SemaphoreType.DMA((len(big) + 2,)),
            pltpu.SemaphoreType.DMA((parts,)),
            pltpu.SemaphoreType.DMA((parts,)),
            pltpu.SemaphoreType.DMA((parts,)),
            pltpu.SemaphoreType.DMA((parts,)),
        ],
        compiler_params=pltpu.CompilerParams(
            collective_id=0, has_side_effects=True, vmem_limit_bytes=56 * 1024 * 1024
        ),
        name="exchange",
    )(*big, short_taps, skip_gain)
    full = jax.ShapeDtypeStruct((tokens, channels), BF16)
    *outs, skip = pl.pallas_call(
        finish_kernel,
        out_shape=(
            full, full, full, full,
            jax.ShapeDtypeStruct((tokens, channels), F32),
            jax.ShapeDtypeStruct(short_taps.shape, F32),
            jax.ShapeDtypeStruct((1, channels), F32),
        ),
        in_specs=[vmem] * 6,
        out_specs=(vmem,) * 7,
        name="finish",
    )(got, one, two, value, out_grad, short_taps)
    return (*outs, skip.reshape(channels))


def solution(mesh):
    rows, lanes = P("seq", "ch"), P("ch")
    taps = P(None, None, "ch")
    return jax.shard_map(
        functools.partial(per_device, ROWS_Z),
        mesh=mesh,
        in_specs=(rows, rows, rows, rows, taps, lanes, rows),
        out_specs=(rows, rows, rows, rows, rows, taps, lanes),
        check_vma=False,
    )
```

```python
import functools
import math

import jax
import jax.numpy as jnp
import numpy as np
from jax import lax
from jax.experimental import pallas as pl
from jax.experimental.pallas import tpu as pltpu
from jax.sharding import PartitionSpec as P

MESH = pl.DeviceIdType.MESH
F32 = jnp.float32
BF16 = jnp.bfloat16
LANES = 128
ROWS_Z = 16
HALO_LATER, HALO_SOONER, SUMS, FIELD = 0, 6, 12, 32


def halves(table):
    high = table.astype(BF16)
    low = (table - high.astype(np.float64)).astype(BF16)
    return high, low


def tables(devices, tokens, own):
    length = 2 * devices * tokens
    a = np.arange(devices)
    b = np.arange(tokens)
    odd = np.arange(devices) + 0.5
    outer = 2 * math.pi * np.outer(odd, a) / (2 * devices)
    first = np.concatenate([np.cos(outer), -np.sin(outer)], 0)
    last = np.concatenate([np.cos(outer.T), np.sin(outer.T)], 1) * (2.0 / length)
    turn = 2 * math.pi * np.outer(odd, b) / length
    inner = 2 * math.pi * (np.outer(b, b) % tokens) / tokens
    cosine, sine = np.cos(inner), np.sin(inner)
    second = np.block([[cosine, -sine], [sine, cosine]])
    order = np.zeros((own * devices, own * devices))
    for c in range(own):
        order[c * devices + a, a * own + c] = 1.0
    return (
        np.concatenate(halves(first), 0),
        np.stack(halves(last)),
        np.stack([np.cos(turn), -np.sin(turn)]).astype(np.float32),
        np.stack(halves(second)),
        np.stack([order, order.T]).astype(BF16),
    )


def split(x):
    high = x.astype(BF16)
    return high, (x - high.astype(F32)).astype(BF16)


def mul(a, b):
    return jnp.dot(a, b, preferred_element_type=F32)


def exchange_kernel(
    devices, parts, own, rows_z,
    filter_in, two_in, value_in, one_in, cot_in, first_in, last_in, turn_in, second_in, order_in,
    taps_in, skip_in,
    out_ref,
    filter_ref, two_ref, value_ref, one_ref, cot_ref,
    first_ref, last_ref, turn_ref, second_ref, order_ref,
    taps_ref, skip_ref,
    send, recv, ret,
    load_sem, send_sem, recv_sem, ret_sem, out_sem,
):
    me = lax.axis_index("seq")
    tokens = filter_ref.shape[0]
    rows_x = devices // rows_z
    my_x, my_z = me // rows_z, lax.rem(me, rows_z)

    columns = [lax.rem(my_x + dx, rows_x) * rows_z for dx in (2, 1, 3, 0)]
    middle = rows_z // 2

    def farthest_first(visit):
        def line(dz):
            z = lax.rem(my_z + dz, rows_z)
            for column in columns:
                visit(column + z)

        def both(i, carry):
            line(middle + i)
            line(middle - i)
            return carry

        line(middle)
        lax.fori_loop(1, middle, both, 0)
        for column in columns[:-1]:
            visit(column + my_z)

    barrier = pltpu.get_barrier_semaphore()
    farthest_first(
        lambda d: pl.semaphore_signal(barrier, inc=1, device_id={"seq": d}, device_id_type=MESH)
    )

    inputs = (
        filter_in, two_in, value_in, one_in, cot_in,
        first_in, last_in, turn_in, second_in, order_in, taps_in, skip_in,
    )
    held = (
        filter_ref, two_ref, value_ref, one_ref, cot_ref,
        first_ref, last_ref, turn_ref, second_ref, order_ref, taps_ref, skip_ref,
    )
    loads = [pltpu.make_async_copy(x, y, load_sem.at[i]) for i, (x, y) in enumerate(zip(inputs, held))]
    for load in loads:
        load.start()

    def spread(src, dst, at, ssem, rsem):
        def visit(d):
            pltpu.make_async_remote_copy(
                src.at[d, at], dst.at[me, at], ssem, rsem, device_id={"seq": d}, device_id_type=MESH
            ).start()

        farthest_first(visit)
        pltpu.make_async_copy(src.at[me, at], dst.at[me, at], rsem).start()

    others = pl.ds(0, devices - 1)

    def settle(ref, sem):
        pltpu.make_async_copy(ref, ref, sem).wait()

    for p in range(5):
        loads[p].wait()
        for h in range(parts):
            block = held[p][:, h * LANES : (h + 1) * LANES].T
            send[:, 5 * h + p] = block.reshape(devices, own, tokens)
    pl.semaphore_wait(barrier, devices - 1)
    forth = (pl.ds(0, 6), pl.ds(6, 4))
    outward = (pl.ds(0, 3), pl.ds(3, 4))
    for h in range(parts):
        spread(send, recv, forth[h], send_sem.at[h], recv_sem.at[h])
    for load in loads[5:]:
        load.wait()

    def sent():
        for h in range(parts):
            settle(send.at[others, forth[h]], send_sem.at[h])

    lane = lax.broadcasted_iota(jnp.int32, (devices, tokens), 1)
    row = lax.broadcasted_iota(jnp.int32, (devices, tokens), 0)

    def later(x, j):
        r = pltpu.roll(x, j, 1)
        up = jnp.where(row == 0, 0.0, pltpu.roll(r, 1, 0))
        return jnp.where(lane < j, up, r)

    def short(s, channel, x):
        moved = (x, later(x, 1), later(x, 2))
        total = taps_ref[s, 0, channel] * moved[0]
        total = total + taps_ref[s, 1, channel] * moved[1]
        return total + taps_ref[s, 2, channel] * moved[2], moved

    turn_re, turn_im = turn_ref[0], turn_ref[1]

    def rotate(re, im):
        return re * turn_re - im * turn_im, re * turn_im + im * turn_re

    def mul_second(x):
        high, low = split(x)
        return mul(high, second_ref[0]) + (mul(low, second_ref[0]) + mul(high, second_ref[1]))

    def rows_of(x, i):
        return x[i * devices : (i + 1) * devices]

    def forward(pieces):
        rows = []
        for x in pieces:
            both = mul(first_ref[...], x)
            both = both[: 2 * devices] + both[2 * devices :]
            rows.append(jnp.concatenate(rotate(both[:devices], both[devices:]), 1))
        full = mul_second(jnp.concatenate(rows, 0))
        size = own * devices
        return [
            (full[i * size : (i + 1) * size, :tokens], full[i * size : (i + 1) * size, tokens:])
            for i in range(len(pieces) // own)
        ]

    def inverse(spectra):
        full = mul_second(jnp.concatenate([jnp.concatenate(z, 1) for z in spectra], 0))
        result = []
        for i in range(len(spectra) * own):
            part = rows_of(full, i)
            high, low = split(jnp.concatenate(rotate(part[:, :tokens], part[:, tokens:]), 0))
            result.append(mul(last_ref[0], high) + (mul(last_ref[0], low) + mul(last_ref[1], high)))
        return [result[i * own : (i + 1) * own] for i in range(len(spectra))]

    ones = jnp.ones((tokens, tokens), BF16)

    def gather(h, p):
        x = mul(order_ref[0], recv[:, 5 * h + p].reshape(devices * own, tokens))
        return [rows_of(x, c) for c in range(own)]

    def give(p, pieces):
        stacked = jnp.concatenate([x.astype(BF16) for x in pieces], 0)
        ret[:, p] = mul(order_ref[1], stacked).astype(BF16).reshape(devices, own, tokens)

    each = range(own)
    filters = []
    edges = jnp.zeros((devices, tokens), F32)
    for h in range(parts):
        channels = [h * LANES + own * me + c for c in each]
        skip = [skip_ref[channels[c]] for c in each]
        settle(recv.at[:, forth[h]], recv_sem.at[h])
        fresh = [x.astype(BF16) for k in ((0, 1) if h == 0 else ()) for x in gather(k, 0)]
        two = [short(1, channels[c], x) for c, x in enumerate(gather(h, 1))]
        val = [short(2, channels[c], x) for c, x in enumerate(gather(h, 2))]
        one = [short(0, channels[c], x) for c, x in enumerate(gather(h, 3))]
        cot = gather(h, 4)
        mixed = [(two[c][0] * val[c][0]).astype(BF16) for c in each]
        back = [(cot[c] * one[c][0]).astype(BF16) for c in each]
        (m_re, m_im), (b_re, b_im), *more = forward(mixed + back + fresh)
        filters += more
        f_re, f_im = filters[h]
        conv, grad_mixed, grad_filter = inverse([
            (m_re * f_re - m_im * f_im, -(m_re * f_im + m_im * f_re)),
            (b_re * f_re + b_im * f_im, b_re * f_im - b_im * f_re),
            (b_re * m_re + b_im * m_im, b_re * m_im - b_im * m_re),
        ])
        mixed_wide = [x.astype(F32) for x in mixed]
        long_out = [conv[c] + skip[c] * mixed_wide[c] for c in each]
        give(3 * h, long_out)
        back_wide = [x.astype(F32) for x in back]
        grad_in = [grad_mixed[c] + skip[c] * back_wide[c] for c in each]
        give(3 * h + 1, grad_in)
        give(3 * h + 2, grad_filter)
        if h < parts - 1:
            spread(ret, out_ref, outward[h], ret_sem.at[h], out_sem.at[h])
        sections = []
        for c in each:
            field = FIELD * (own * h + c)
            grads = (cot[c] * long_out[c], grad_in[c] * val[c][0], grad_in[c] * two[c][0])
            streams = (one[c][1], two[c][1], val[c][1])
            for s in range(3):
                at = field + HALO_LATER + 2 * s
                piece = pltpu.roll(streams[s][2], at, 1) if at else streams[s][2]
                edges = jnp.where((lane >= at) & (lane < at + 2), piece, edges)
                at = field + HALO_SOONER + 2 * s
                ahead = jnp.where(row == devices - 1, 0.0, pltpu.roll(grads[s], devices - 1, 0))
                edges = jnp.where((lane >= at) & (lane < at + 2), pltpu.roll(ahead, at, 1), edges)
                for j in range(3):
                    sections.append(grads[s] * streams[s][j])
            sections.append(back_wide[c] * mixed_wide[c])
            sections += [None] * 6
        gathered = [
            jnp.zeros((8, tokens), F32) if x is None else x.reshape(devices // 8, 8, tokens).sum(0)
            for x in sections
        ]
        high, low = split(jnp.concatenate(gathered, 0))
        totals = mul(high, ones) + mul(low, ones)
        section = lax.broadcasted_iota(jnp.int32, totals.shape, 0) // 8
        target = FIELD * (own * h + section // 16) + SUMS + section % 16
        pick = lax.broadcasted_iota(jnp.int32, totals.shape, 1) == target
        edges = edges + jnp.where(pick, totals, 0.0).sum(0, keepdims=True)
    give(3 * parts, split(edges))
    spread(ret, out_ref, outward[-1], ret_sem.at[parts - 1], out_sem.at[parts - 1])

    sent()
    for h in range(parts):
        settle(ret.at[others, outward[h]], ret_sem.at[h])
        settle(out_ref.at[:, outward[h]], out_sem.at[h])


def finish_kernel(
    got_ref, one_ref, two_ref, value_ref, cot_ref, taps_ref,
    mixed_out_ref, grad_one_ref, grad_two_ref, grad_value_ref, filter_ref, taps_out_ref, skip_out_ref,
):
    devices, units, own, tokens = got_ref.shape
    parts = units // 3
    source = lax.broadcasted_iota(jnp.int32, (LANES, LANES), 0)
    target = lax.broadcasted_iota(jnp.int32, (LANES, LANES), 1)
    row = lax.broadcasted_iota(jnp.int32, (tokens, LANES), 0)

    def turn(p):
        return got_ref[:, p].reshape(LANES, tokens).T

    turned = turn(3 * parts)
    for h in range(parts):
        at = slice(h * LANES, (h + 1) * LANES)
        long_out, grad_in, grad_filter = [turn(3 * h + p) for p in range(3)]
        long_out, grad_in = long_out.astype(F32), grad_in.astype(F32)
        edges = jnp.zeros((FIELD, LANES), F32)
        for c in range(own):
            place = jnp.where((source // own == target // own) & (target % own == c), 1.0, 0.0)
            field = FIELD * (own * h + c)
            edges = edges + mul(turned[field : field + FIELD], place.astype(BF16))

        def edge(i):
            return edges[i : i + 1]

        def tap(s, j):
            return taps_ref[s, j : j + 1, at]

        gates = []
        for s, ref in enumerate((one_ref, two_ref, value_ref)):
            x = ref[:, at].astype(F32)
            i = HALO_LATER + 2 * s
            once = jnp.where(row == 0, edge(i + 1), pltpu.roll(x, 1, 0))
            twice = jnp.where(row == 0, edge(i), jnp.where(row == 1, edge(i + 1), pltpu.roll(x, 2, 0)))
            total = tap(s, 0) * x
            total = total + tap(s, 1) * once
            gates.append(total + tap(s, 2) * twice)
        mixed_out_ref[:, at] = (gates[0] * long_out).astype(BF16)
        grads = (cot_ref[:, at].astype(F32) * long_out, grad_in * gates[2], grad_in * gates[1])
        for s, ref in enumerate((grad_one_ref, grad_two_ref, grad_value_ref)):
            x = grads[s]
            i = HALO_SOONER + 2 * s
            once = jnp.where(row == tokens - 1, edge(i), pltpu.roll(x, tokens - 1, 0))
            twice = pltpu.roll(x, tokens - 2, 0)
            twice = jnp.where(row == tokens - 1, edge(i + 1), jnp.where(row == tokens - 2, edge(i), twice))
            total = tap(s, 0) * x
            total = total + tap(s, 1) * once
            ref[:, at] = (total + tap(s, 2) * twice).astype(BF16)
        filter_ref[:, at] = grad_filter.astype(F32)
        for s in range(3):
            taps_out_ref[s, :, at] = edges[SUMS + 3 * s : SUMS + 3 * s + 3]
        skip_out_ref[:, at] = edges[SUMS + 9 : SUMS + 10]


def per_device(rows_z, one, two, value, long_filter, short_taps, skip_gain, out_grad):
    devices = lax.axis_size("seq")
    tokens, channels = one.shape
    parts = channels // LANES
    own = LANES // devices
    anywhere = pl.BlockSpec(memory_space=pl.ANY)
    vmem = pl.BlockSpec(memory_space=pltpu.VMEM)
    consts = [jnp.asarray(t) for t in tables(devices, tokens, own)]
    big = (long_filter, two, value, one, out_grad, *consts)
    inward = (devices, 5 * parts, own, tokens)
    outward = (devices, 3 * parts + 1, own, tokens)
    got = pl.pallas_call(
        functools.partial(exchange_kernel, devices, parts, own, rows_z),
        out_shape=jax.ShapeDtypeStruct(outward, BF16),
        in_specs=[anywhere] * (len(big) + 2),
        out_specs=anywhere,
        scratch_shapes=[pltpu.VMEM(x.shape, x.dtype) for x in big]
        + [
            pltpu.SMEM(short_taps.shape, F32),
            pltpu.SMEM(skip_gain.shape, F32),
            pltpu.VMEM(inward, BF16),
            pltpu.VMEM(inward, BF16),
            pltpu.VMEM(outward, BF16),
            pltpu.SemaphoreType.DMA((len(big) + 2,)),
            pltpu.SemaphoreType.DMA((parts,)),
            pltpu.SemaphoreType.DMA((parts,)),
            pltpu.SemaphoreType.DMA((parts,)),
            pltpu.SemaphoreType.DMA((parts,)),
        ],
        compiler_params=pltpu.CompilerParams(
            collective_id=0, has_side_effects=True, vmem_limit_bytes=56 * 1024 * 1024
        ),
        name="exchange",
    )(*big, short_taps, skip_gain)
    full = jax.ShapeDtypeStruct((tokens, channels), BF16)
    *outs, skip = pl.pallas_call(
        finish_kernel,
        out_shape=(
            full, full, full, full,
            jax.ShapeDtypeStruct((tokens, channels), F32),
            jax.ShapeDtypeStruct(short_taps.shape, F32),
            jax.ShapeDtypeStruct((1, channels), F32),
        ),
        in_specs=[vmem] * 6,
        out_specs=(vmem,) * 7,
        name="finish",
    )(got, one, two, value, out_grad, short_taps)
    return (*outs, skip.reshape(channels))


def solution(mesh):
    rows, lanes = P("seq", "ch"), P("ch")
    taps = P(None, None, "ch")
    return jax.shard_map(
        functools.partial(per_device, ROWS_Z),
        mesh=mesh,
        in_specs=(rows, rows, rows, rows, taps, lanes, rows),
        out_specs=(rows, rows, rows, rows, rows, taps, lanes),
        check_vma=False,
    )
```
